32 devices in a mesh: dp: 8 (over y, x, core), expert: 4 (over z).
Axes of the slice: x: 2, y: 2, z: 4, core: 2. Of those that a mesh axis runs over, the one named last changes fastest.
Arguments:
- tokens: bfloat16 [512, 2048], P(('dp', 'expert')), may hold values from -6 to 6
- route: int32 [512, 8], P(('dp', 'expert')), may hold values from 0 to 15, all different within a row; in each aligned block of 16 rows (0 to 15, 16 to 31, ...) at most 12 rows name the same one
- probs: float32 [512, 8], P(('dp', 'expert')), may hold values from 0.03 to 0.3
- cotangent: bfloat16 [512, 2048], P(('dp', 'expert')), may hold values from -6 to 6
- gate_weight: bfloat16 [32, 2048, 384], P(('dp', 'expert')), may hold values from -0.125 to 0.125
- up_weight: bfloat16 [32, 2048, 384], P(('dp', 'expert')), may hold values from -0.125 to 0.125
- down_weight: bfloat16 [32, 384, 2048], P(('dp', 'expert')), may hold values from -0.21875 to 0.21875
Outputs:
- mixed: bfloat16 [512, 2048], P(('dp', 'expert'))
- token_grad: bfloat16 [512, 2048], P(('dp', 'expert'))
- gate_grad: bfloat16 [32, 2048, 384], P(('dp', 'expert'))
- up_grad: bfloat16 [32, 2048, 384], P(('dp', 'expert'))
- down_grad: bfloat16 [32, 384, 2048], P(('dp', 'expert'))
The draws below stay inside these ranges and needn't reach their ends.
Inputs may be any that keep to these rules, and one draw needn't show every extreme that they name: `route`: each row names 8 different experts. In each aligned block of 16 rows (the rows of one device) no expert is named by more than 12 rows, a bound that some block reaches.
All inputs are finite; a program needn't handle non-finite values.
Results may differ from the reference program's by a relative error of at most 0.0065.
Values may be sent and summed in bfloat16 or wider, within the bound.
No kernel may reach another device: no remote copies, remote signals or barrier semaphores. Data moves between devices by JAX's collectives and lax.ppermute only.
A program may use at most 64 MiB of HBM per device.

```python
import math
import jax
import jax.numpy as jnp
import numpy as np
from jax import lax

D = 2048
HID = 768
TOP = 8
TOK_DEV = 16
DEVICES_ALL = 32
EXPERTS = 16
HSLICE = 384
CAP = 12
TOKENS = 512
N_DP = 8
N_EXPERT = 4


def steps_of(key, extent, split, smallest, high):
    loudness = 1.0
    for dim, parts in split:
        steps = jax.random.uniform(jax.random.fold_in(jax.random.fold_in(key, 6), dim), (parts,), jnp.float32, smallest / len(split), high / len(split))
        loudness = loudness * jnp.repeat(jnp.exp(steps), extent[dim] // parts).reshape((-1,) + (1,) * (len(extent) - 1 - dim))
    return loudness


def deal_out(own_key, own, number, rows, number_of, top, limit, slope):
    order = jax.random.permutation(own_key, number_of)
    packed, common = load_shares(number_of, rows * top, limit, slope, True), load_shares(number_of, rows * top, limit, slope, False)
    places = jnp.arange(number_of)

    def named(lengths, turn):
        used = int((lengths > 0).sum())
        fixed = max(1, used // 4)
        passed = fixed + (places - fixed + turn * (used - fixed)) % max(1, number_of - fixed)
        return jnp.zeros((number_of,), jnp.int32).at[order[jnp.where(places < fixed, places, passed)]].set(jnp.asarray(lengths, jnp.int32))

    lengths = jnp.where(number % 4 == 0, named(packed, number // 4), named(common, number - number // 4 - 1))
    mixed = jax.random.permutation(jax.random.fold_in(own, 3), number_of)
    donor, taker = mixed[0:number_of // 2 * 2:2], mixed[1:number_of // 2 * 2:2]
    room = jnp.minimum(lengths[donor] - 1, limit - lengths[taker]) // 2
    room = jnp.where((donor == order[0]) | (taker == order[0]) | (lengths[taker] == 0), 0, jnp.maximum(room, 0))
    passed = jax.random.randint(jax.random.fold_in(own, 4), (number_of // 2,), 0, 1 << 20) % (room + 1)
    lengths = lengths.at[donor].add(-passed).at[taker].add(passed)
    members = jnp.searchsorted(jnp.cumsum(lengths), jnp.arange(rows * top), side="right").astype(jnp.int32)
    grid = members.reshape(top, rows).T
    grid = grid[jax.random.permutation(jax.random.fold_in(own, 1), rows)]
    turn = jax.random.randint(jax.random.fold_in(own, 2), (rows, 1), 0, top)
    return jnp.take_along_axis(grid, (jnp.arange(top)[None, :] + turn) % top, axis=1)


def load_shares(number_of, total, reach, lean, full):
    portions = [(1 << 20) // math.isqrt(grade ** lean) + 1 for grade in range(1, number_of + 1)]
    largest = reach if full else min(reach, max(-(-total // number_of), total * portions[0] // sum(portions)))
    least = 1 if total - largest >= number_of - 1 else 0
    given, spare = [largest] + [least] * (number_of - 1), total - largest - least * (number_of - 1)
    while spare > 0:
        movable = [i for i in range(1, number_of) if given[i] < largest] or [i for i in range(1, number_of) if given[i] < reach]
        mass, remaining = sum([portions[i] for i in movable]), spare
        for i in movable:
            extra = min(reach - given[i], max(1, remaining * portions[i] // mass), spare)
            given[i] = given[i] + extra
            spare = spare - extra
    return np.array(given)


def noise(stream_key, shape, width, reach, cuts=(), kind=jnp.bfloat16):
    loudness = steps_of(stream_key, shape, cuts, -0.22, 0.18) if cuts else 1.0
    drawn = jax.random.normal(stream_key, shape, jnp.float32) * width * loudness
    return jnp.minimum(jnp.maximum(drawn, -reach), reach).astype(kind)


def setup_inputs(seed: int = 0) -> dict:
    key_of = jax.random.split(jax.random.key(seed), 8)
    tokens = noise(key_of[0], (TOKENS, D), 1.0, 6.0, ((0, 32),))
    route_keys = jax.random.split(jax.random.fold_in(key_of[1], 1), TOKENS // TOK_DEV)
    route_turns = jax.random.permutation(jax.random.fold_in(key_of[1], 3), TOKENS // TOK_DEV)
    route = jax.vmap(lambda own, number: deal_out(jax.random.fold_in(key_of[1], 2), own, number, TOK_DEV, EXPERTS, TOP, CAP, 2))(route_keys, route_turns).reshape((TOKENS, TOP))
    probs = jnp.clip(jnp.exp(math.log(0.3) - 2.3025852 * jax.random.uniform(key_of[2], (TOKENS, TOP), jnp.float32) ** steps_of(key_of[2], (TOKENS, TOP), ((0, 32),), -0.2, 0.2)), 0.03, 0.3)
    cotangent = noise(key_of[3], (TOKENS, D), 1.0, 6.0, ((0, 32),))
    gate_weight = noise(key_of[4], (DEVICES_ALL, D, HSLICE), D ** -0.5, 0.125, ((0, 32),))
    up_weight = noise(key_of[5], (DEVICES_ALL, D, HSLICE), D ** -0.5, 0.125, ((0, 32),))
    down_weight = noise(key_of[6], (DEVICES_ALL, HSLICE, D), HID ** -0.5, 0.21875, ((0, 32),))
    return {"tokens": tokens, "route": route, "probs": probs, "cotangent": cotangent, "gate_weight": gate_weight, "up_weight": up_weight, "down_weight": down_weight}


def slot_tables(route_block, prob_block, experts, capacity):
    row_count, top_count = route_block.shape
    flat_ids = route_block.reshape(-1)
    onehot = (flat_ids[:, None] == jnp.arange(experts, dtype=jnp.int32)[None, :]).astype(jnp.int32)
    before = jnp.cumsum(onehot, axis=0) - onehot
    position = jnp.sum(before * onehot, axis=1).astype(jnp.int32)
    slot_ids = (flat_ids * capacity + position).astype(jnp.int32)
    matches = (slot_ids[:, None] == jnp.arange(experts * capacity, dtype=jnp.int32)[None, :]).astype(jnp.float32)
    matches = matches.reshape(row_count, top_count, experts * capacity)
    return jnp.sum(matches, axis=1), jnp.sum(matches * prob_block[:, :, None].astype(jnp.float32), axis=1)


def rounded(values):
    return lax.optimization_barrier(values.astype(jnp.bfloat16)).astype(jnp.float32)


def reference(tokens, route, probs, cotangent, gate_weight, up_weight, down_weight):
    highest = lax.Precision.HIGHEST
    device_count = N_DP * N_EXPERT
    hslice = HID // 2
    gate_full = gate_weight.reshape(EXPERTS, 2, D, hslice).transpose(0, 2, 1, 3).reshape(EXPERTS, D, HID)
    up_full = up_weight.reshape(EXPERTS, 2, D, hslice).transpose(0, 2, 1, 3).reshape(EXPERTS, D, HID)
    down_full = down_weight.reshape(EXPERTS, HID, D)
    token_all = tokens.reshape(device_count, TOK_DEV, D).astype(jnp.float32)
    cot_all = cotangent.reshape(device_count, TOK_DEV, D).astype(jnp.float32)
    spread, weighted = jax.vmap(lambda a, b: slot_tables(a, b, EXPERTS, CAP))(
        route.reshape(device_count, TOK_DEV, TOP), probs.reshape(device_count, TOK_DEV, TOP))
    spread = spread.reshape(device_count, TOK_DEV, EXPERTS, CAP)
    weighted = weighted.reshape(device_count, TOK_DEV, EXPERTS, CAP)

    def one_expert(totals, index):
        spread_part = lax.dynamic_index_in_dim(spread, index, 2, keepdims=False)
        weight_part = lax.dynamic_index_in_dim(weighted, index, 2, keepdims=False)
        w_gate = lax.dynamic_index_in_dim(gate_full, index, 0, keepdims=False).astype(jnp.float32)
        w_up = lax.dynamic_index_in_dim(up_full, index, 0, keepdims=False).astype(jnp.float32)
        w_down = lax.dynamic_index_in_dim(down_full, index, 0, keepdims=False).astype(jnp.float32)
        slot_rows = rounded(jnp.einsum('ntc,ntd->ncd', spread_part, token_all, precision=highest)).reshape(-1, D)
        out_cot = rounded(jnp.einsum('ntc,ntd->ncd', weight_part, cot_all, precision=highest)).reshape(-1, D)
        gate_val = jnp.dot(slot_rows, w_gate, precision=highest)
        up_val = jnp.dot(slot_rows, w_up, precision=highest)
        sigmoid_val = jax.nn.sigmoid(gate_val)
        act_val = rounded(gate_val * sigmoid_val * up_val)
        out_rows = rounded(jnp.dot(act_val, w_down, precision=highest))
        act_cot = jnp.einsum('rd,hd->rh', out_cot, w_down, precision=highest)
        gate_cot = rounded(act_cot * up_val * sigmoid_val * (1.0 + gate_val * (1.0 - sigmoid_val)))
        up_cot = rounded(act_cot * gate_val * sigmoid_val)
        grad_down = jnp.einsum('rh,rd->hd', act_val, out_cot, precision=highest)
        grad_gate = jnp.einsum('rd,rh->dh', slot_rows, gate_cot, precision=highest)
        grad_up = jnp.einsum('rd,rh->dh', slot_rows, up_cot, precision=highest)
        rows_cot = rounded(jnp.einsum('rh,dh->rd', gate_cot, w_gate, precision=highest)
                           + jnp.einsum('rh,dh->rd', up_cot, w_up, precision=highest))
        out_rows = out_rows.reshape(device_count, CAP, D)
        rows_cot = rows_cot.reshape(device_count, CAP, D)
        mixed_acc = totals[0] + jnp.einsum('ntc,ncd->ntd', weight_part, out_rows, precision=highest)
        token_acc = totals[1] + jnp.einsum('ntc,ncd->ntd', spread_part, rows_cot, precision=highest)
        gate_slices = grad_gate.reshape(D, 2, hslice).transpose(1, 0, 2)
        up_slices = grad_up.reshape(D, 2, hslice).transpose(1, 0, 2)
        down_slices = grad_down.reshape(2, hslice, D)
        return (mixed_acc, token_acc), (gate_slices.astype(jnp.bfloat16), up_slices.astype(jnp.bfloat16),
                                        down_slices.astype(jnp.bfloat16))

    zeros = jnp.zeros((device_count, TOK_DEV, D), jnp.float32)
    (mixed_acc, token_acc), grads = lax.scan(one_expert, (zeros, zeros), jnp.arange(EXPERTS, dtype=jnp.int32))
    mixed = mixed_acc.reshape(TOKENS, D).astype(jnp.bfloat16)
    token_grad = token_acc.reshape(TOKENS, D).astype(jnp.bfloat16)
    gate_grad = grads[0].reshape(device_count, D, hslice)
    up_grad = grads[1].reshape(device_count, D, hslice)
    down_grad = grads[2].reshape(device_count, hslice, D)
    return mixed, token_grad, gate_grad, up_grad, down_grad
```

```python
import jax
import jax.numpy as jnp
from jax import lax
from jax.sharding import PartitionSpec as P

AXES = ("dp", "expert")
F32, BF16 = jnp.float32, jnp.bfloat16


def permutes(n_dp, n_ex):
    def pairs(to):
        out = []
        for d in range(n_dp):
            for z in range(n_ex):
                e, y = to(d, z)
                out.append((d * n_ex + z, e * n_ex + y))
        return out

    def mixed(step, bits):
        def to(d, z):
            bit = step if d % 2 == 0 else bits - 1 - step
            return d ^ (2 << bit), z

        return pairs(to)

    bits = n_dp.bit_length() - 2
    core = pairs(lambda d, z: (d ^ 1, z))
    plane = [mixed(s, bits) for s in range(bits)]
    both, back_both = [], []
    for j in range(1, n_ex - 1, 2):
        both.append(pairs(lambda d, z, j=j: (d, (z + j + d % 2) % n_ex)))
        back_both.append(pairs(lambda d, z, j=j: (d, (z - j - d % 2) % n_ex)))
    last = pairs(lambda d, z: (d, (z + n_ex - 1) % n_ex))
    back_last = pairs(lambda d, z: (d, (z + 1) % n_ex))
    return core, plane, both, back_both, last, back_last


def send(x, pairs):
    return lax.ppermute(x, AXES, pairs)


def gather_lane(own, perms):
    core, plane, both, _, last, _ = perms
    chip = jnp.concatenate((own, send(own, core)))
    lane = [own] + [send(chip, p) for p in both] + [send(own, last)]
    lane = jnp.concatenate(lane)
    for p in plane:
        lane = jnp.concatenate((lane, send(lane, p)))
    return lane


def add(a, b):
    return a.astype(F32) + b.astype(F32)


def reduce_back(kept, given, rows, perms):
    core, plane, _, back_both, _, back_last = perms
    lane = add(kept, send(given, core))
    for p in reversed(plane):
        lane = lane.astype(BF16)
        half = lane.shape[0] // 2
        lane = add(lane[:half], send(lane[half:], p))
    lane = lane.astype(BF16)
    total = lane[:rows].astype(F32)
    given = jnp.zeros_like(total)
    at = rows
    for p in back_both:
        back = send(lane[at : at + 2 * rows], p).astype(F32)
        total, given = total + back[:rows], given + back[rows:]
        at += 2 * rows
    total = total + send(lane[at:], back_last).astype(F32)
    return (total + send(given, core)).astype(BF16)


def contract_last(left, right):
    return lax.dot_general(left, right, (((1,), (1,)), ((), ())), preferred_element_type=F32)


def contract_first(left, right):
    return lax.dot_general(left, right, (((0,), (0,)), ((), ())), preferred_element_type=F32)


def dot(left, right):
    return jnp.dot(left, right, preferred_element_type=F32)


def weight_table(route, probs, experts):
    hit = route[:, :, None] == jnp.arange(experts, dtype=jnp.int32)
    table = jnp.sum(jnp.where(hit, probs[:, :, None], 0.0), axis=1)
    parts = []
    for _ in range(3):
        part = lax.reduce_precision(table, 8, 7)
        parts.append(part.astype(BF16))
        table = table - part
    table = jnp.concatenate(parts, axis=1)
    return jnp.pad(table, ((0, 0), (0, -table.shape[1] % 128)))


def body(tokens, route, probs, cotangent, gate_weight, up_weight, down_weight):
    n_dp, n_ex = lax.axis_size("dp"), lax.axis_size("expert")
    experts = n_dp * n_ex // 2
    rows, width = tokens.shape
    perms = permutes(n_dp, n_ex)
    core = perms[0]
    w_gate, w_up, w_down = gate_weight[0], up_weight[0], down_weight[0]

    lane_rows = gather_lane(jnp.concatenate((tokens, weight_table(route, probs, experts)), axis=1), perms)
    lane_cot = gather_lane(cotangent, perms)
    all_rows = jnp.concatenate((lane_rows, send(lane_rows, core)))
    all_cot = jnp.concatenate((lane_cot, send(lane_cot, core)))

    expert = (lax.axis_index("dp") * n_ex + lax.axis_index("expert")) // 2
    table = all_rows[:, width:].astype(F32)
    columns = jnp.arange(table.shape[1], dtype=jnp.int32)
    mine = (columns % experts == expert) & (columns < 3 * experts)
    p = jnp.sum(jnp.where(mine, table, 0.0), axis=1, keepdims=True)
    x = all_rows[:, :width]
    out_cot = (p * all_cot.astype(F32)).astype(BF16)

    gate_val, up_val = dot(x, w_gate), dot(x, w_up)
    s = jax.nn.sigmoid(gate_val)
    act = (gate_val * s * up_val).astype(BF16)
    half = act.shape[0] // 2
    mixed = reduce_back(
        (p[:half] * dot(act[:half], w_down)).astype(BF16),
        (p[half:] * dot(act[half:], w_down)).astype(BF16),
        rows,
        perms,
    )
    act_cot = contract_last(out_cot, w_down)
    gate_cot = (act_cot * up_val * s * (1.0 + gate_val * (1.0 - s))).astype(BF16)
    up_cot = (act_cot * gate_val * s).astype(BF16)
    kept, given = (
        (contract_last(g, w_gate) + contract_last(u, w_up)).astype(BF16)
        for g, u in ((gate_cot[:half], up_cot[:half]), (gate_cot[half:], up_cot[half:]))
    )
    token_grad = reduce_back(kept, given, rows, perms)
    return (
        mixed,
        token_grad,
        contract_first(x, gate_cot).astype(BF16)[None],
        contract_first(x, up_cot).astype(BF16)[None],
        contract_first(act, out_cot).astype(BF16)[None],
    )


def solution(mesh):
    two, three = P(AXES, None), P(AXES, None, None)
    return jax.shard_map(
        body,
        mesh=mesh,
        in_specs=(two, two, two, two, three, three, three),
        out_specs=(two, two, three, three, three),
        check_vma=False,
    )
```

```python
import functools

import jax
import jax.numpy as jnp
from jax import lax
from jax.experimental import pallas as pl
from jax.experimental.pallas import tpu as pltpu
from jax.sharding import PartitionSpec as P

AXES = ("dp", "expert")
F32, BF16 = jnp.float32, jnp.bfloat16
BLOCK = 128


def permutes(n_dp, n_ex):
    def pairs(to):
        out = []
        for d in range(n_dp):
            for z in range(n_ex):
                e, y = to(d, z)
                out.append((d * n_ex + z, e * n_ex + y))
        return out

    def mixed(step, bits):
        def to(d, z):
            bit = step if d % 2 == 0 else bits - 1 - step
            return d ^ (2 << bit), z

        return pairs(to)

    bits = n_dp.bit_length() - 2
    core = pairs(lambda d, z: (d ^ 1, z))
    plane = [mixed(s, bits) for s in range(bits)]
    line = [pairs(lambda d, z, j=j: (d, (z + j) % n_ex)) for j in range(1, n_ex)]
    back = [pairs(lambda d, z, j=j: (d, (z - j) % n_ex)) for j in range(1, n_ex)]
    return core, plane, line, back


def send(x, pairs):
    return lax.ppermute(x, AXES, pairs)


def after(x, *others):
    return lax.optimization_barrier((x, *others))[0]


def add(*terms):
    return functools.reduce(lambda a, b: a + b, [t.astype(F32) for t in terms])


def nt(left, right):
    return lax.dot_general(left, right, (((1,), (1,)), ((), ())), preferred_element_type=F32)


def tn(left, right):
    return lax.dot_general(left, right, (((0,), (0,)), ((), ())), preferred_element_type=F32)


def dot(left, right):
    return jnp.dot(left, right, preferred_element_type=F32)


def shaped(*arrays):
    return [jax.ShapeDtypeStruct(s, t) for s, t in arrays]


def params(mib):
    return pltpu.CompilerParams(vmem_limit_bytes=mib << 20)


def cost(microseconds):
    return pl.CostEstimate(flops=int(microseconds * 1.15e9), bytes_accessed=0, transcendentals=0)


WHOLE = pl.BlockSpec(memory_space=pltpu.VMEM)
ANY = pl.BlockSpec(memory_space=pltpu.HBM)


def payload_kernel(experts, tokens, cotangent, route_in, probs_in, out, cot, route, probs, sems):
    rows, width = tokens.shape
    copies = [
        pltpu.make_async_copy(a, b, sems.at[i])
        for i, (a, b) in enumerate(
            ((route_in, route), (probs_in, probs), (tokens, out.at[:, :width]), (cotangent, cot))
        )
    ]
    for copy in copies:
        copy.start()
    for copy in copies[:2]:
        copy.wait()
    extra = out.shape[1] - width
    column = lax.broadcasted_iota(jnp.int32, (extra, rows), 0)
    named, part = column, jnp.zeros_like(column)
    for _ in range(2):
        over = named >= experts
        named, part = jnp.where(over, named - experts, named), part + over.astype(jnp.int32)
    table = jnp.zeros((extra, rows), F32)
    for k in range(route.shape[0]):
        table = table + jnp.where(route[k : k + 1, :] == named, probs[k : k + 1, :], 0.0)
    high = table.astype(BF16).astype(F32)
    middle = (table - high).astype(BF16).astype(F32)
    low = table - high - middle
    table = jnp.where(part == 0, high, jnp.where(part == 1, middle, low))
    out[:, width:] = jnp.transpose(table).astype(BF16)
    for copy in copies[2:]:
        copy.wait()


def payload(tokens, cotangent, route, probs, experts):
    rows, width = tokens.shape
    extra = -(-3 * experts // 128) * 128
    return pl.pallas_call(
        functools.partial(payload_kernel, experts),
        in_specs=[ANY] * 4,
        out_specs=[WHOLE] * 2,
        out_shape=[pltpu.VMEM((rows, width + extra), BF16), pltpu.VMEM((rows, width), BF16)],
        scratch_shapes=[
            pltpu.VMEM(route.shape[::-1], jnp.int32),
            pltpu.VMEM(probs.shape[::-1], F32),
            pltpu.SemaphoreType.DMA((4,)),
        ],
        compiler_params=params(60),
    )(tokens, cotangent, route.T, probs.T)


def stage_kernel(*refs):
    count = len(refs) // 2
    copies = [pltpu.make_async_copy(refs[i], refs[count + i], refs[-1].at[i]) for i in range(count)]
    for copy in copies:
        copy.start()
    for copy in copies:
        copy.wait()


def stage(*arrays):
    return pl.pallas_call(
        stage_kernel,
        in_specs=[ANY] * len(arrays),
        out_specs=[WHOLE] * len(arrays),
        out_shape=[pltpu.VMEM(a.shape, a.dtype) for a in arrays],
        scratch_shapes=[pltpu.SemaphoreType.DMA((len(arrays),))],
        compiler_params=params(50),
    )(*arrays)


def join_kernel(*refs):
    at = 0
    for ref in refs[:-1]:
        refs[-1][at : at + ref.shape[0], :] = ref[...]
        at += ref.shape[0]


def join(*arrays, length=0.0):
    rows = sum(a.shape[0] for a in arrays)
    return pl.pallas_call(
        join_kernel,
        in_specs=[WHOLE] * len(arrays),
        out_specs=WHOLE,
        out_shape=pltpu.VMEM((rows, arrays[0].shape[1]), BF16),
        compiler_params=params(4),
        cost_estimate=cost(length),
    )(*arrays)


def grid_specs(block, arrays, whole):
    specs = [pl.BlockSpec((block * f, w), lambda i: (i, 0)) for f, w in arrays]
    return specs + [pl.BlockSpec(w.shape, lambda i: (0, 0, 0)) for w in whole]


def over_rows(kernel, n, scalars, taken, weights, given, length=0.0):
    block = min(n, BLOCK)
    if block == n:
        call = dict(in_specs=[WHOLE] * (len(taken) + len(weights)), out_specs=[WHOLE] * len(given))
    else:
        call = dict(
            grid=(n // block,),
            in_specs=grid_specs(block, [(f, a.shape[1]) for f, a in taken], weights),
            out_specs=grid_specs(block, [(f, w) for f, w, _ in given], []),
        )
    call["in_specs"] = [pl.BlockSpec(memory_space=pltpu.SMEM)] * len(scalars) + call["in_specs"]
    return pl.pallas_call(
        kernel,
        out_shape=shaped(*[((f * n, w), t) for f, w, t in given]),
        compiler_params=params(12 if block == n else 40),
        cost_estimate=cost(length),
        **call,
    )(*scalars, *[a for _, a in taken], *weights)


def expert_weight(experts, expert, table):
    column = lax.broadcasted_iota(jnp.int32, table.shape, 1)
    mine = expert[0, 0]
    mine = (column == mine) | (column == mine + experts) | (column == mine + 2 * experts)
    return jnp.sum(jnp.where(mine, table.astype(F32), 0.0), axis=1, keepdims=True)


def hidden_units(x, w_gate, w_up, act, gate_f, up_f):
    gate, up = dot(x, w_gate[0]), dot(x, w_up[0])
    s = jax.nn.sigmoid(gate)
    gate_s = gate * s
    act_val = (gate_s * up).astype(BF16)
    act[...] = act_val
    up_f[...] = gate_s
    gate_f[...] = up * s * (1.0 + gate * (1.0 - s))
    return act_val


def forward_pair_kernel(experts, expert, a, b, w_gate, w_up, w_down, kept, given, act, gate_f, up_f, weight):
    n, width = a.shape[0], w_gate.shape[1]
    x = jnp.concatenate((a[:, :width], b[:, :width]))
    p = expert_weight(experts, expert, jnp.concatenate((a[:, width:], b[:, width:])))
    weight[...] = jnp.broadcast_to(p, weight.shape)
    act_val = hidden_units(x, w_gate, w_up, act, gate_f, up_f)
    out = p * dot(act_val, w_down[0])
    kept[...] = out[:n].astype(BF16)
    given[...] = out[n:].astype(BF16)


def forward_pair(a, b, weights, expert, experts, length=0.0):
    width, hidden = weights[0].shape[1:]
    given = [(1, width, BF16)] * 2 + [(2, hidden, BF16), (2, hidden, F32), (2, hidden, F32), (2, 128, F32)]
    kernel = functools.partial(forward_pair_kernel, experts)
    return over_rows(kernel, a.shape[0], [expert], [(1, a), (1, b)], weights, given, length)


def forward_hidden_kernel(experts, expert, a, w_gate, w_up, act, gate_f, up_f, weight):
    width = w_gate.shape[1]
    weight[...] = jnp.broadcast_to(expert_weight(experts, expert, a[:, width:]), weight.shape)
    hidden_units(a[:, :width], w_gate, w_up, act, gate_f, up_f)


def forward_out_kernel(act, weight, w_down, out):
    out[...] = (weight[:, :1] * dot(act[...], w_down[0])).astype(BF16)


def forward_full_kernel(experts, expert, a, w_gate, w_up, w_down, act, gate_f, up_f, weight, out):
    width = w_gate.shape[1]
    p = expert_weight(experts, expert, a[:, width:])
    weight[...] = jnp.broadcast_to(p, weight.shape)
    act_val = hidden_units(a[:, :width], w_gate, w_up, act, gate_f, up_f)
    out[...] = (p * dot(act_val, w_down[0])).astype(BF16)


def forward_one(kernel, a, weights, expert, experts, outs, length=0.0):
    width, hidden = weights[0].shape[1:]
    given = [(1, hidden, BF16), (1, hidden, F32), (1, hidden, F32), (1, 128, F32)] + [(1, width, BF16)] * outs
    return over_rows(functools.partial(kernel, experts), a.shape[0], [expert], [(1, a)], weights, given, length)


def hidden_cots(cot, weight, gate_f, up_f, w_down, gate_cot, up_cot, out_cot):
    out = (cot.astype(F32) * weight[:, :1]).astype(BF16)
    out_cot[...] = out
    act_cot = nt(out, w_down[0])
    gate = (act_cot * gate_f[...]).astype(BF16)
    up = (act_cot * up_f[...]).astype(BF16)
    gate_cot[...], up_cot[...] = gate, up
    return gate, up


def row_cots(gate, up, w_gate, w_up):
    return nt(gate, w_gate[0]) + nt(up, w_up[0])


def backward_pair_kernel(a, b, weight, gate_f, up_f, w_gate, w_up, w_down, kept, given, gate_cot, up_cot, out_cot):
    n = a.shape[0]
    cot = jnp.concatenate((a[...], b[...]))
    gate, up = hidden_cots(cot, weight, gate_f, up_f, w_down, gate_cot, up_cot, out_cot)
    part = row_cots(gate, up, w_gate, w_up)
    kept[...] = part[:n].astype(BF16)
    given[...] = part[n:].astype(BF16)


def backward_pair(a, b, weight, gate_f, up_f, weights, length=0.0):
    n, width = a.shape
    hidden = weights[0].shape[2]
    taken = [(1, a), (1, b), (2, weight), (2, gate_f), (2, up_f)]
    given = [(1, width, BF16)] * 2 + [(2, hidden, BF16)] * 2 + [(2, width, BF16)]
    return over_rows(backward_pair_kernel, n, [], taken, weights, given, length)


def backward_hidden_kernel(cot, weight, gate_f, up_f, w_down, gate_cot, up_cot, out_cot):
    hidden_cots(cot[...], weight, gate_f, up_f, w_down, gate_cot, up_cot, out_cot)


def backward_rows_kernel(gate, up, w_gate, w_up, out):
    out[...] = row_cots(gate[...], up[...], w_gate, w_up).astype(BF16)


def backward_full_kernel(cot, weight, gate_f, up_f, w_gate, w_up, w_down, gate_cot, up_cot, out_cot, out):
    gate, up = hidden_cots(cot[...], weight, gate_f, up_f, w_down, gate_cot, up_cot, out_cot)
    out[...] = row_cots(gate, up, w_gate, w_up).astype(BF16)


def backward_one(kernel, cot, weight, gate_f, up_f, weights, outs, length=0.0):
    n, width = cot.shape
    hidden = gate_f.shape[1]
    taken = [(1, cot), (1, weight), (1, gate_f), (1, up_f)]
    given = [(1, hidden, BF16)] * 2 + [(1, width, BF16)] * (1 + outs)
    return over_rows(kernel, n, [], taken, weights, given, length)


def gradient_kernel(width, counts, *refs):
    joined = []
    for count in counts:
        joined.append(jnp.concatenate([r[...] for r in refs[:count]]))
        refs = refs[count:]
    outs, total = refs[:-1], refs[-1]
    part = tn(joined[0][:, :width], jnp.concatenate(joined[1:], axis=1))

    def write(value):
        hidden = value.shape[1] // len(outs)
        for i, out in enumerate(outs):
            out[0] = value[:, i * hidden : (i + 1) * hidden].astype(BF16)

    if total.shape[0] == 8:
        write(part)
        return
    step = pl.program_id(0)

    @pl.when(step == 0)
    def _():
        total[...] = part

    @pl.when(step > 0)
    def _():
        total[...] += part

    @pl.when(step == pl.num_programs(0) - 1)
    def _():
        write(total[...])


def gradients(left, rights, width, steps):
    hidden = rights[0][0].shape[1]
    groups = [left, *rights]
    flat = [piece for group in groups for piece in group]
    if steps == 1:
        specs = [WHOLE] * len(flat)
    else:
        specs = [pl.BlockSpec((a.shape[0] // steps, a.shape[1]), lambda i: (i, 0)) for a in flat]
    total = (8, 128) if steps == 1 else (width, len(rights) * hidden)
    return pl.pallas_call(
        functools.partial(gradient_kernel, width, [len(g) for g in groups]),
        grid=(steps,),
        in_specs=specs,
        out_specs=[pl.BlockSpec((1, width, hidden), lambda i: (0, 0, 0))] * len(rights),
        out_shape=shaped(*[((1, width, hidden), BF16)] * len(rights)),
        scratch_shapes=[pltpu.VMEM(total, F32)],
        compiler_params=params(24 if steps == 1 else 48),
        cost_estimate=cost(10.0),
    )(*flat)


def body(tokens, route, probs, cotangent, gate_weight, up_weight, down_weight):
    n_dp, n_ex = lax.axis_size("dp"), lax.axis_size("expert")
    experts = n_dp * n_ex // 2
    rows, width = tokens.shape
    core, plane, line, back = permutes(n_dp, n_ex)
    expert = lax.shift_right_logical(lax.axis_index(AXES).astype(jnp.int32), 1).reshape(1, 1)
    expert, tokens = lax.optimization_barrier((expert, tokens))

    own, cot = payload(tokens, cotangent, route, probs, experts)
    row_lane = join(own, *[send(own, p) for p in line])
    weights = (gate_weight, up_weight, down_weight)
    if row_lane.shape[0] * 2 <= BLOCK:
        weights = stage(*(after(w, row_lane) for w in weights))
    w_gate, w_up, w_down = weights
    cot_lane = join(after(cot, w_gate), *[send(cot, p) for p in line], length=10.0)
    for p in plane[:-2]:
        row_lane = join(row_lane, send(row_lane, p))
        cot_lane = join(cot_lane, send(cot_lane, p))
    row_lane = join(row_lane, after(send(row_lane, plane[-2]), cot_lane))
    row_late = send(row_lane, plane[-1])
    row_other = send(row_lane, core)
    f_early = forward_pair(row_lane, row_other, weights, expert, experts, 10.0)
    cot_lane = join(cot_lane, after(send(cot_lane, plane[-2]), f_early[0]))
    cot_late = send(cot_lane, plane[-1])
    cot_other = send(cot_lane, core)

    def halve(kept, received):
        return add(kept, received).astype(BF16)

    row_late = after(row_late, cot_lane)
    row_late_other = send(row_late, core)
    f_own = forward_one(forward_hidden_kernel, row_late, (w_gate, w_up), expert, experts, 0, 10.0)
    f_other = forward_one(forward_full_kernel, row_late_other, weights, expert, experts, 1, 10.0)
    o_other = send(f_other[4], core)
    (o_own,) = over_rows(
        forward_out_kernel, row_late.shape[0], [], [(1, f_own[0]), (1, after(f_own[3], f_other[0]))], (w_down,), [(1, width, BF16)], 10.0
    )
    o_late = halve(o_own, o_other)
    o_early_other = send(f_early[1], core)
    o_back = send(o_late, plane[-1])

    cot_late = after(cot_late, o_late)
    cot_late_other = send(cot_late, core)
    b_own = backward_one(backward_hidden_kernel, cot_late, f_own[3], f_own[1], f_own[2], (w_down,), 0, 10.0)
    b_other = backward_one(
        backward_full_kernel, cot_late_other, f_other[3], f_other[1], f_other[2], weights, 1, 10.0
    )
    g_other = send(b_other[3], core)
    (g_own,) = over_rows(
        backward_rows_kernel, cot_late.shape[0], [], [(1, b_own[0]), (1, after(b_own[1], b_other[0]))], (w_gate, w_up), [(1, width, BF16)], 10.0
    )
    g_late = halve(g_own, g_other)
    cot_other = after(cot_other, g_late)
    b_early = backward_pair(cot_lane, cot_other, f_early[5], f_early[3], f_early[4], weights, 10.0)
    g_early_other = send(b_early[1], core)
    g_back = send(g_late, plane[-1])
    o_back = after(o_back, g_late)

    def finish(lane):
        for p in reversed(plane[:-1]):
            half = lane.shape[0] // 2
            lane = halve(lane[:half], send(lane[half:], p))
        terms = [lane[:rows]]
        for j, p in enumerate(back, 1):
            terms.append(send(lane[j * rows : (j + 1) * rows], p))
        return add(*terms).astype(BF16)

    mixed = finish(add(f_early[0], o_early_other, o_back).astype(BF16))
    token_grad = finish(add(b_early[0], g_early_other, g_back).astype(BF16))

    steps = max(1, row_late.shape[0] // BLOCK)
    lefts = [after(row_lane, g_late), row_other, row_late, row_late_other]
    gate_cots, up_cots, out_cots = zip(b_early[2:5], b_own[:3], b_other[:3])
    gate_grad, up_grad = gradients(lefts, [gate_cots, up_cots], width, steps)
    (down_grad,) = gradients([after(f_early[2], g_late), f_own[0], f_other[0]], [out_cots], f_own[0].shape[1], steps)
    return mixed, token_grad, gate_grad, up_grad, down_grad


def solution(mesh):
    two, three = P(AXES, None), P(AXES, None, None)
    return jax.shard_map(
        body,
        mesh=mesh,
        in_specs=(two, two, two, two, three, three, three),
        out_specs=(two, two, three, three, three),
        check_vma=False,
    )
```

```python
import functools

import jax
import jax.numpy as jnp
from jax import lax
from jax.experimental import pallas as pl
from jax.experimental.pallas import tpu as pltpu
from jax.sharding import PartitionSpec as P

AXES = ("dp", "expert")
F32, BF16 = jnp.float32, jnp.bfloat16
BLOCK = 128


def permutes(n_dp, n_ex):
    def pairs(to):
        out = []
        for d in range(n_dp):
            for z in range(n_ex):
                e, y = to(d, z)
                out.append((d * n_ex + z, e * n_ex + y))
        return out

    def mixed(step, bits):
        def to(d, z):
            bit = step if d % 2 == 0 else bits - 1 - step
            return d ^ (2 << bit), z

        return pairs(to)

    bits = n_dp.bit_length() - 2
    core = pairs(lambda d, z: (d ^ 1, z))
    plane = [mixed(s, bits) for s in range(bits)]
    line = [pairs(lambda d, z, j=j: (d, z ^ j)) for j in reversed(range(1, n_ex))]
    return core, plane, line


def send(x, pairs):
    return lax.ppermute(x, AXES, pairs)


def after(x, *others):
    return lax.optimization_barrier((x, *others))[0]


def add(*terms):
    return functools.reduce(lambda a, b: a + b, [t.astype(F32) for t in terms])


def nt(left, right):
    return lax.dot_general(left, right, (((1,), (1,)), ((), ())), preferred_element_type=F32)


def tn(left, right):
    return lax.dot_general(left, right, (((0,), (0,)), ((), ())), preferred_element_type=F32)


def dot(left, right):
    return jnp.dot(left, right, preferred_element_type=F32)


def shaped(*arrays):
    return [jax.ShapeDtypeStruct(s, t) for s, t in arrays]


def params(mib):
    return pltpu.CompilerParams(vmem_limit_bytes=mib << 20)


def cost(microseconds):
    return pl.CostEstimate(flops=int(microseconds * 1.15e9), bytes_accessed=0, transcendentals=0)


WHOLE = pl.BlockSpec(memory_space=pltpu.VMEM)
ANY = pl.BlockSpec(memory_space=pltpu.HBM)


def payload_kernel(experts, tokens, cotangent, route_in, probs_in, out, cot, route, probs, sems):
    rows, width = tokens.shape
    copies = [
        pltpu.make_async_copy(a, b, sems.at[i])
        for i, (a, b) in enumerate(
            ((route_in, route), (probs_in, probs), (tokens, out.at[:, :width]), (cotangent, cot))
        )
    ]
    for copy in copies:
        copy.start()
    for copy in copies[:2]:
        copy.wait()
    extra = out.shape[1] - width
    column = lax.broadcasted_iota(jnp.int32, (extra, rows), 0)
    named, part = column, jnp.zeros_like(column)
    for _ in range(2):
        over = named >= experts
        named, part = jnp.where(over, named - experts, named), part + over.astype(jnp.int32)
    table = jnp.zeros((extra, rows), F32)
    for k in range(route.shape[0]):
        table = table + jnp.where(route[k : k + 1, :] == named, probs[k : k + 1, :], 0.0)
    high = table.astype(BF16).astype(F32)
    middle = (table - high).astype(BF16).astype(F32)
    low = table - high - middle
    table = jnp.where(part == 0, high, jnp.where(part == 1, middle, low))
    out[:, width:] = jnp.transpose(table).astype(BF16)
    for copy in copies[2:]:
        copy.wait()


def payload(tokens, cotangent, route, probs, experts):
    rows, width = tokens.shape
    extra = -(-3 * experts // 128) * 128
    return pl.pallas_call(
        functools.partial(payload_kernel, experts),
        in_specs=[ANY] * 4,
        out_specs=[WHOLE] * 2,
        out_shape=[pltpu.VMEM((rows, width + extra), BF16), pltpu.VMEM((rows, width), BF16)],
        scratch_shapes=[
            pltpu.VMEM(route.shape[::-1], jnp.int32),
            pltpu.VMEM(probs.shape[::-1], F32),
            pltpu.SemaphoreType.DMA((4,)),
        ],
        compiler_params=params(60),
    )(tokens, cotangent, route.T, probs.T)


def stage_kernel(gate, up, down, tall, wide, sems):
    copies = [
        pltpu.make_async_copy(a.at[0], b, sems.at[i])
        for i, (a, b) in enumerate(((gate, tall.at[0]), (up, tall.at[1]), (down, wide.at[2])))
    ]
    for copy in copies:
        copy.start()
    for i, copy in enumerate(copies):
        copy.wait()
        if i < 2:
            wide[i] = jnp.transpose(tall[i])
        else:
            tall[i] = jnp.transpose(wide[i])


def stage(gate, up, down):
    _, width, hidden = gate.shape
    return pl.pallas_call(
        stage_kernel,
        in_specs=[ANY] * 3,
        out_specs=[WHOLE] * 2,
        out_shape=[pltpu.VMEM((3, width, hidden), BF16), pltpu.VMEM((3, hidden, width), BF16)],
        scratch_shapes=[pltpu.SemaphoreType.DMA((3,))],
        compiler_params=params(52),
    )(gate, up, down)


class Weights:
    def __init__(self, refs):
        self.refs = refs
        self.staged = len(refs) == 2

    def hidden(self, x):
        if self.staged:
            return dot(x, self.refs[0][0]), dot(x, self.refs[0][1])
        return dot(x, self.refs[0][0]), dot(x, self.refs[1][0])

    def out(self, act):
        return dot(act, self.refs[1][2] if self.staged else self.refs[2][0])

    def act_cot(self, out_cot):
        return dot(out_cot, self.refs[0][2]) if self.staged else nt(out_cot, self.refs[2][0])

    def row_cot(self, gate, up):
        if self.staged:
            return dot(gate, self.refs[1][0]) + dot(up, self.refs[1][1])
        return nt(gate, self.refs[0][0]) + nt(up, self.refs[1][0])


def join_kernel(*refs):
    at = 0
    for ref in refs[:-1]:
        refs[-1][at : at + ref.shape[0], :] = ref[...]
        at += ref.shape[0]


def join(*arrays, length=0.0):
    rows = sum(a.shape[0] for a in arrays)
    return pl.pallas_call(
        join_kernel,
        in_specs=[WHOLE] * len(arrays),
        out_specs=WHOLE,
        out_shape=pltpu.VMEM((rows, arrays[0].shape[1]), BF16),
        compiler_params=params(4),
        cost_estimate=cost(length),
    )(*arrays)


def grid_specs(block, arrays, whole):
    specs = [pl.BlockSpec((block * f, w), lambda i: (i, 0)) for f, w in arrays]
    return specs + [pl.BlockSpec(w.shape, lambda i: (0, 0, 0)) for w in whole]


def over_rows(kernel, n, scalars, taken, weights, given, length=0.0):
    block = min(n, BLOCK)
    if block == n:
        call = dict(in_specs=[WHOLE] * (len(taken) + len(weights)), out_specs=[WHOLE] * len(given))
    else:
        call = dict(
            grid=(n // block,),
            in_specs=grid_specs(block, [(f, a.shape[1]) for f, a in taken], weights),
            out_specs=grid_specs(block, [(f, w) for f, w, _ in given], []),
        )
    call["in_specs"] = [pl.BlockSpec(memory_space=pltpu.SMEM)] * len(scalars) + call["in_specs"]
    first = len(scalars) + len(taken)

    def run(*refs):
        kernel(*refs[:first], Weights(refs[first : first + len(weights)]), *refs[first + len(weights) :])

    return pl.pallas_call(
        run,
        out_shape=shaped(*[((f * n, w), t) for f, w, t in given]),
        compiler_params=params(12 if block == n else 40),
        cost_estimate=cost(length),
        **call,
    )(*scalars, *[a for _, a in taken], *weights)


def expert_weight(experts, expert, table):
    column = lax.broadcasted_iota(jnp.int32, table.shape, 1)
    mine = expert[0, 0]
    mine = (column == mine) | (column == mine + experts) | (column == mine + 2 * experts)
    return jnp.sum(jnp.where(mine, table.astype(F32), 0.0), axis=1, keepdims=True)


def hidden_units(x, weights, act, gate_f, up_f):
    gate, up = weights.hidden(x)
    s = jax.nn.sigmoid(gate)
    gate_s = gate * s
    act_val = (gate_s * up).astype(BF16)
    act[...] = act_val
    up_f[...] = gate_s
    gate_f[...] = up * s * (1.0 + gate * (1.0 - s))
    return act_val


def forward_pair_kernel(experts, width, expert, a, b, weights, kept, given, act, gate_f, up_f, weight):
    n = a.shape[0]
    x = jnp.concatenate((a[:, :width], b[:, :width]))
    p = expert_weight(experts, expert, jnp.concatenate((a[:, width:], b[:, width:])))
    weight[...] = jnp.broadcast_to(p, weight.shape)
    out = p * weights.out(hidden_units(x, weights, act, gate_f, up_f))
    kept[...] = out[:n].astype(BF16)
    given[...] = out[n:].astype(BF16)


def forward_hidden_kernel(experts, width, expert, a, weights, act, gate_f, up_f, weight):
    weight[...] = jnp.broadcast_to(expert_weight(experts, expert, a[:, width:]), weight.shape)
    hidden_units(a[:, :width], weights, act, gate_f, up_f)


def forward_out_kernel(act, weight, weights, out):
    out[...] = (weight[:, :1] * weights.out(act[...])).astype(BF16)


def forward_full_kernel(experts, width, expert, a, weights, act, gate_f, up_f, weight, out):
    p = expert_weight(experts, expert, a[:, width:])
    weight[...] = jnp.broadcast_to(p, weight.shape)
    act_val = hidden_units(a[:, :width], weights, act, gate_f, up_f)
    out[...] = (p * weights.out(act_val)).astype(BF16)


def hidden_cots(cot, weight, gate_f, up_f, weights, gate_cot, up_cot, out_cot):
    out = (cot.astype(F32) * weight[:, :1]).astype(BF16)
    out_cot[...] = out
    act_cot = weights.act_cot(out)
    gate = (act_cot * gate_f[...]).astype(BF16)
    up = (act_cot * up_f[...]).astype(BF16)
    gate_cot[...], up_cot[...] = gate, up
    return gate, up


def backward_pair_kernel(a, b, weight, gate_f, up_f, weights, kept, given, gate_cot, up_cot, out_cot):
    n = a.shape[0]
    cot = jnp.concatenate((a[...], b[...]))
    part = weights.row_cot(*hidden_cots(cot, weight, gate_f, up_f, weights, gate_cot, up_cot, out_cot))
    kept[...] = part[:n].astype(BF16)
    given[...] = part[n:].astype(BF16)


def backward_hidden_kernel(cot, weight, gate_f, up_f, weights, gate_cot, up_cot, out_cot):
    hidden_cots(cot[...], weight, gate_f, up_f, weights, gate_cot, up_cot, out_cot)


def backward_rows_kernel(gate, up, weights, out):
    out[...] = weights.row_cot(gate[...], up[...]).astype(BF16)


def backward_full_kernel(cot, weight, gate_f, up_f, weights, gate_cot, up_cot, out_cot, out):
    gate, up = hidden_cots(cot[...], weight, gate_f, up_f, weights, gate_cot, up_cot, out_cot)
    out[...] = weights.row_cot(gate, up).astype(BF16)


def chunk_kernel(over_left, chunks, counts, *refs):
    outs = len(counts) - 1
    joined = []
    for count in counts:
        joined.append(refs[:count])
        refs = refs[count:]
    results, held, sems = refs[:outs], refs[outs:-1], refs[-1]
    split = 0 if over_left else 1
    rest = [None if i == split else jnp.concatenate([r[...] for r in group]) for i, group in enumerate(joined)]
    if over_left:
        right = jnp.concatenate(rest[1:], axis=1)
    size = held[0].shape[split] // chunks
    copies = []
    for i in range(chunks):
        part = pl.ds(i * size, size)
        piece = jnp.concatenate([r[:, part] for r in joined[split]])
        value = tn(piece, right) if over_left else tn(rest[0], piece)
        for j in range(outs):
            width = value.shape[1] // outs
            at = (part, slice(None)) if over_left else (slice(None), part)
            held[j][at] = value[:, j * width : (j + 1) * width].astype(BF16)
            copy = pltpu.make_async_copy(held[j].at[at], results[j].at[(0, *at)], sems.at[i, j])
            copy.start()
            copies.append(copy)
    for copy in copies:
        copy.wait()


def gradients_by_chunks(left, rights, width, over_left, chunks=4):
    hidden = rights[0][0].shape[1]
    groups = [left, *rights]
    flat = [piece for group in groups for piece in group]
    return pl.pallas_call(
        functools.partial(chunk_kernel, over_left, chunks, [len(g) for g in groups]),
        in_specs=[WHOLE] * len(flat),
        out_specs=[ANY] * len(rights),
        out_shape=shaped(*[((1, width, hidden), BF16)] * len(rights)),
        scratch_shapes=[pltpu.VMEM((width, hidden), BF16)] * len(rights) + [pltpu.SemaphoreType.DMA((chunks, len(rights)))],
        compiler_params=params(16),
        cost_estimate=cost(10.0),
    )(*flat)


def gradient_kernel(width, counts, *refs):
    joined = []
    for count in counts:
        joined.append(jnp.concatenate([r[...] for r in refs[:count]]))
        refs = refs[count:]
    outs, total = refs[:-1], refs[-1]
    part = tn(joined[0][:, :width], jnp.concatenate(joined[1:], axis=1))

    def write(value):
        hidden = value.shape[1] // len(outs)
        for i, out in enumerate(outs):
            out[0] = value[:, i * hidden : (i + 1) * hidden].astype(BF16)

    if total.shape[0] == 8:
        write(part)
        return
    step = pl.program_id(0)

    @pl.when(step == 0)
    def _():
        total[...] = part

    @pl.when(step > 0)
    def _():
        total[...] += part

    @pl.when(step == pl.num_programs(0) - 1)
    def _():
        write(total[...])


def gradients(left, rights, width, steps):
    hidden = rights[0][0].shape[1]
    if steps == 1:
        over_left = width > hidden
        if max(width, hidden) % (4 * 128) == 0:
            return gradients_by_chunks(left, rights, width, over_left)
    groups = [left, *rights]
    flat = [piece for group in groups for piece in group]
    if steps == 1:
        specs = [WHOLE] * len(flat)
    else:
        specs = [pl.BlockSpec((a.shape[0] // steps, a.shape[1]), lambda i: (i, 0)) for a in flat]
    total = (8, 128) if steps == 1 else (width, len(rights) * hidden)
    return pl.pallas_call(
        functools.partial(gradient_kernel, width, [len(g) for g in groups]),
        grid=(steps,),
        in_specs=specs,
        out_specs=[pl.BlockSpec((1, width, hidden), lambda i: (0, 0, 0))] * len(rights),
        out_shape=shaped(*[((1, width, hidden), BF16)] * len(rights)),
        scratch_shapes=[pltpu.VMEM(total, F32)],
        compiler_params=params(24 if steps == 1 else 48),
        cost_estimate=cost(10.0),
    )(*flat)


def body(tokens, route, probs, cotangent, gate_weight, up_weight, down_weight):
    n_dp, n_ex = lax.axis_size("dp"), lax.axis_size("expert")
    experts = n_dp * n_ex // 2
    rows, width = tokens.shape
    hidden = gate_weight.shape[2]
    core, plane, line = permutes(n_dp, n_ex)
    expert = lax.shift_right_logical(lax.axis_index(AXES).astype(jnp.int32), 1).reshape(1, 1)
    expert, tokens = lax.optimization_barrier((expert, tokens))
    units = [(hidden, BF16), (hidden, F32), (hidden, F32), (128, F32)]
    cots = [(hidden, BF16), (hidden, BF16), (width, BF16)]
    wide = (1, width, BF16)

    def each(factor, arrays):
        return [(factor, *a) for a in arrays]

    own, cot = payload(tokens, cotangent, route, probs, experts)
    weights = (gate_weight, up_weight, down_weight)
    staged = n_ex * rows * 2 <= BLOCK
    if staged:
        weights = stage(*(after(w, own) for w in weights))
    row_lane = join(after(own, weights[0]), *[send(own, p) for p in line])
    cot = after(cot, row_lane)
    cot_lane = join(cot, *[send(cot, p) for p in line], length=10.0)
    for p in plane[:-2]:
        row_lane = join(row_lane, send(row_lane, p))
        cot_lane = join(cot_lane, send(cot_lane, p))
    row_lane = join(row_lane, send(row_lane, plane[-2]))
    n = row_lane.shape[0]
    row_late = send(row_lane, plane[-1])
    row_other = send(row_lane, core)

    def forward(kernel, *args):
        return functools.partial(kernel, experts, width), n, [expert], *args

    f_early = over_rows(
        *forward(forward_pair_kernel, [(1, row_lane), (1, row_other)], weights, [wide] * 2 + each(2, units))
    )
    kept, given, *f_early = f_early
    cot_lane = join(cot_lane, after(send(cot_lane, plane[-2]), kept))
    cot_late = send(cot_lane, plane[-1])
    cot_other = send(cot_lane, core)

    def halve(kept, received):
        return add(kept, received).astype(BF16)

    row_late = after(row_late, cot_lane)
    row_late_other = send(row_late, core)
    f_own = over_rows(*forward(forward_hidden_kernel, [(1, row_late)], weights, each(1, units), 10.0))
    *f_other, o_given = over_rows(
        *forward(forward_full_kernel, [(1, row_late_other)], weights, each(1, units) + [wide], 10.0)
    )
    o_other = send(o_given, core)
    taken = [(1, f_own[0]), (1, after(f_own[3], f_other[0]))]
    (o_own,) = over_rows(forward_out_kernel, n, [], taken, weights, [wide], 10.0)
    o_late = halve(o_own, o_other)
    o_early_other = send(given, core)
    o_back = send(o_late, plane[-1])

    def with_units(cot, factor, f):
        return [(factor, f[3]), (factor, f[1]), (factor, f[2])]

    cot_late = after(cot_late, o_late)
    cot_late_other = send(cot_late, core)
    taken = [(1, cot_late)] + with_units(cot_late, 1, f_own)
    b_own = over_rows(backward_hidden_kernel, n, [], taken, weights, each(1, cots), 10.0)
    taken = [(1, cot_late_other)] + with_units(cot_late_other, 1, f_other)
    *b_other, g_given = over_rows(backward_full_kernel, n, [], taken, weights, each(1, cots) + [wide], 10.0)
    g_other = send(g_given, core)
    taken = [(1, b_own[0]), (1, after(b_own[1], b_other[0]))]
    (g_own,) = over_rows(backward_rows_kernel, n, [], taken, weights, [wide], 10.0)
    g_late = halve(g_own, g_other)
    cot_other = after(cot_other, g_late)
    taken = [(1, cot_lane), (1, cot_other)] + with_units(cot_lane, 2, f_early)
    g_kept, g_given, *b_early = over_rows(
        backward_pair_kernel, n, [], taken, weights, [wide] * 2 + each(2, cots), 10.0
    )
    g_early_other = send(g_given, core)
    g_back = send(g_late, plane[-1])
    o_back = after(o_back, g_late)

    def finish(lane):
        for p in reversed(plane[:-1]):
            half = lane.shape[0] // 2
            lane = halve(lane[:half], send(lane[half:], p))
        terms = [lane[:rows]]
        for j, p in enumerate(line, 1):
            terms.append(send(lane[j * rows : (j + 1) * rows], p))
        return add(*terms).astype(BF16)

    mixed = finish(add(kept, o_early_other, o_back).astype(BF16))
    token_grad = finish(add(g_kept, g_early_other, g_back).astype(BF16))

    steps = max(1, n // BLOCK)
    lefts = [after(row_lane, g_late), row_other, row_late, row_late_other]
    gate_cots, up_cots, out_cots = zip(b_early, b_own, b_other)
    gate_grad, up_grad = gradients(lefts, [gate_cots, up_cots], width, steps)
    acts = [after(f_early[0], g_late), f_own[0], f_other[0]]
    (down_grad,) = gradients(acts, [out_cots], hidden, steps)
    return mixed, token_grad, gate_grad, up_grad, down_grad


def solution(mesh):
    two, three = P(AXES, None), P(AXES, None, None)
    return jax.shard_map(
        body,
        mesh=mesh,
        in_specs=(two, two, two, two, three, three, three),
        out_specs=(two, two, three, three, three),
        check_vma=False,
    )
```

```python
import functools

import jax
import jax.numpy as jnp
from jax import lax
from jax.experimental import pallas as pl
from jax.experimental.pallas import tpu as pltpu
from jax.sharding import PartitionSpec as P

AXES = ("dp", "expert")
F32, BF16 = jnp.float32, jnp.bfloat16
BLOCK = 128


def permutes(n_dp, n_ex):
    def pairs(to):
        out = []
        for d in range(n_dp):
            for z in range(n_ex):
                e, y = to(d, z)
                out.append((d * n_ex + z, e * n_ex + y))
        return out

    def mixed(step, bits):
        def to(d, z):
            bit = step if d % 2 == 0 else bits - 1 - step
            return d ^ (2 << bit), z

        return pairs(to)

    bits = n_dp.bit_length() - 2
    core = pairs(lambda d, z: (d ^ 1, z))
    plane = [mixed(s, bits) for s in range(bits)]
    line = [pairs(lambda d, z, j=j: (d, z ^ j)) for j in reversed(range(1, n_ex))]
    return core, plane, line


def send(x, pairs):
    return lax.ppermute(x, AXES, pairs)


def after(x, *others):
    return lax.optimization_barrier((x, *others))[0]


def add(*terms):
    return functools.reduce(lambda a, b: a + b, [t.astype(F32) for t in terms])


def nt(left, right):
    return lax.dot_general(left, right, (((1,), (1,)), ((), ())), preferred_element_type=F32)


def tn(left, right):
    return lax.dot_general(left, right, (((0,), (0,)), ((), ())), preferred_element_type=F32)


def dot(left, right):
    return jnp.dot(left, right, preferred_element_type=F32)


def shaped(*arrays):
    return [jax.ShapeDtypeStruct(s, t) for s, t in arrays]


def params(mib):
    return pltpu.CompilerParams(vmem_limit_bytes=mib << 20)


def cost(microseconds):
    return pl.CostEstimate(flops=int(microseconds * 1.15e9), bytes_accessed=0, transcendentals=0)


WHOLE = pl.BlockSpec(memory_space=pltpu.VMEM)
ANY = pl.BlockSpec(memory_space=pltpu.HBM)


def payload_kernel(experts, tokens, cotangent, route_in, probs_in, out, cot, route, probs, sems):
    rows, width = tokens.shape
    copies = [
        pltpu.make_async_copy(a, b, sems.at[i])
        for i, (a, b) in enumerate(
            ((route_in, route), (probs_in, probs), (tokens, out.at[:, :width]), (cotangent, cot))
        )
    ]
    for copy in copies:
        copy.start()
    for copy in copies[:2]:
        copy.wait()
    extra = out.shape[1] - width
    column = lax.broadcasted_iota(jnp.int32, (extra, rows), 0)
    named, part = column, jnp.zeros_like(column)
    for _ in range(2):
        over = named >= experts
        named, part = jnp.where(over, named - experts, named), part + over.astype(jnp.int32)
    table = jnp.zeros((extra, rows), F32)
    for k in range(route.shape[0]):
        table = table + jnp.where(route[k : k + 1, :] == named, probs[k : k + 1, :], 0.0)
    high = table.astype(BF16).astype(F32)
    middle = (table - high).astype(BF16).astype(F32)
    low = table - high - middle
    table = jnp.where(part == 0, high, jnp.where(part == 1, middle, low))
    out[:, width:] = jnp.transpose(table).astype(BF16)
    for copy in copies[2:]:
        copy.wait()


def payload(tokens, cotangent, route, probs, experts):
    rows, width = tokens.shape
    extra = -(-3 * experts // 128) * 128
    return pl.pallas_call(
        functools.partial(payload_kernel, experts),
        in_specs=[ANY] * 4,
        out_specs=[WHOLE] * 2,
        out_shape=[pltpu.VMEM((rows, width + extra), BF16), pltpu.VMEM((rows, width), BF16)],
        scratch_shapes=[
            pltpu.VMEM(route.shape[::-1], jnp.int32),
            pltpu.VMEM(probs.shape[::-1], F32),
            pltpu.SemaphoreType.DMA((4,)),
        ],
        compiler_params=params(60),
    )(tokens, cotangent, route.T, probs.T)


def stage_kernel(gate, up, down, tall, wide, sems):
    copies = [
        pltpu.make_async_copy(a.at[0], b, sems.at[i])
        for i, (a, b) in enumerate(((gate, tall.at[0]), (up, tall.at[1]), (down, wide.at[2])))
    ]
    for copy in copies:
        copy.start()
    for i, copy in enumerate(copies):
        copy.wait()
        if i < 2:
            wide[i] = jnp.transpose(tall[i])
        else:
            tall[i] = jnp.transpose(wide[i])


def stage(gate, up, down):
    _, width, hidden = gate.shape
    return pl.pallas_call(
        stage_kernel,
        in_specs=[ANY] * 3,
        out_specs=[WHOLE] * 2,
        out_shape=[pltpu.VMEM((3, width, hidden), BF16), pltpu.VMEM((3, hidden, width), BF16)],
        scratch_shapes=[pltpu.SemaphoreType.DMA((3,))],
        compiler_params=params(52),
    )(gate, up, down)


class Weights:
    def __init__(self, refs):
        self.refs = refs
        self.staged = len(refs) == 2

    def hidden(self, x):
        if self.staged:
            return dot(x, self.refs[0][0]), dot(x, self.refs[0][1])
        return dot(x, self.refs[0][0]), dot(x, self.refs[1][0])

    def out(self, act):
        return dot(act, self.refs[1][2] if self.staged else self.refs[2][0])

    def act_cot(self, out_cot):
        return dot(out_cot, self.refs[0][2]) if self.staged else nt(out_cot, self.refs[2][0])

    def row_cot(self, gate, up):
        if self.staged:
            return dot(gate, self.refs[1][0]) + dot(up, self.refs[1][1])
        return nt(gate, self.refs[0][0]) + nt(up, self.refs[1][0])


def join_kernel(blocks, *refs):
    at, out = 0, refs[-1]
    for i in range(blocks):
        for ref in refs[:-1]:
            size = ref.shape[0] // blocks
            out[at : at + size, :] = ref[i * size : (i + 1) * size, :]
            at += size


def join(*arrays, blocks=1, length=0.0):
    rows = sum(a.shape[0] for a in arrays)
    return pl.pallas_call(
        functools.partial(join_kernel, blocks),
        in_specs=[WHOLE] * len(arrays),
        out_specs=WHOLE,
        out_shape=pltpu.VMEM((rows, arrays[0].shape[1]), BF16),
        compiler_params=params(4),
        cost_estimate=cost(length),
    )(*arrays)


def split_sum_kernel(blocks, *refs):
    arrays, outs = refs[:-2], refs[-2:]
    half = outs[0].shape[0] // blocks
    for i in range(blocks):
        for j, out in enumerate(outs):
            rows = pl.ds((2 * i + j) * half, half)
            total = functools.reduce(lambda x, y: x + y, [r[rows, :].astype(F32) for r in arrays])
            out[i * half : (i + 1) * half, :] = total.astype(BF16)


def split_sum(blocks, *arrays):
    rows, width = arrays[0].shape
    return pl.pallas_call(
        functools.partial(split_sum_kernel, blocks),
        in_specs=[WHOLE] * len(arrays),
        out_specs=[WHOLE] * 2,
        out_shape=[pltpu.VMEM((rows // 2, width), BF16)] * 2,
        compiler_params=params(4),
        cost_estimate=cost(0.0),
    )(*arrays)


def grid_specs(block, arrays, whole):
    specs = [pl.BlockSpec((block * f, w), lambda i: (i, 0)) for f, w in arrays]
    return specs + [pl.BlockSpec(w.shape, lambda i: (0, 0, 0)) for w in whole]


def last_sums_kernel(counts, *refs):
    taken, results, held, sems = refs[: sum(counts)], refs[-5:-3], refs[-3:-1], refs[-1]
    copies = []
    for i, count in enumerate(counts):
        total = functools.reduce(lambda x, y: x + y, [r[...].astype(F32) for r in taken[:count]])
        taken = taken[count:]
        held[i][...] = total.astype(BF16)
        copies.append(pltpu.make_async_copy(held[i], results[i], sems.at[i]))
        copies[i].start()
    for copy in copies:
        copy.wait()


def last_sums(*groups):
    shape = groups[0][0].shape
    return pl.pallas_call(
        functools.partial(last_sums_kernel, [len(g) for g in groups]),
        in_specs=[WHOLE] * sum(len(g) for g in groups),
        out_specs=[ANY] * len(groups),
        out_shape=shaped(*[(shape, BF16)] * len(groups)),
        scratch_shapes=[pltpu.VMEM(shape, BF16)] * len(groups) + [pltpu.SemaphoreType.DMA((len(groups),))],
        compiler_params=params(4),
        cost_estimate=cost(0.0),
    )(*[a for g in groups for a in g])


def over_rows(kernel, n, scalars, taken, weights, given, length=0.0):
    block = min(n, BLOCK)
    if block == n:
        call = dict(in_specs=[WHOLE] * (len(taken) + len(weights)), out_specs=[WHOLE] * len(given))
    else:
        call = dict(
            grid=(n // block,),
            in_specs=grid_specs(block, [(f, a.shape[1]) for f, a in taken], weights),
            out_specs=grid_specs(block, [(f, w) for f, w, _ in given], []),
        )
    call["in_specs"] = [pl.BlockSpec(memory_space=pltpu.SMEM)] * len(scalars) + call["in_specs"]
    first = len(scalars) + len(taken)

    def run(*refs):
        kernel(*refs[:first], Weights(refs[first : first + len(weights)]), *refs[first + len(weights) :])

    return pl.pallas_call(
        run,
        out_shape=shaped(*[((f * n, w), t) for f, w, t in given]),
        compiler_params=params(12 if block == n else 40),
        cost_estimate=cost(length),
        **call,
    )(*scalars, *[a for _, a in taken], *weights)


def expert_weight(experts, expert, table):
    column = lax.broadcasted_iota(jnp.int32, table.shape, 1)
    mine = expert[0, 0]
    mine = (column == mine) | (column == mine + experts) | (column == mine + 2 * experts)
    return jnp.sum(jnp.where(mine, table.astype(F32), 0.0), axis=1, keepdims=True)


def hidden_values(x, weights):
    gate, up = weights.hidden(x)
    s = jax.nn.sigmoid(gate)
    gate_s = gate * s
    return (gate_s * up).astype(BF16), up * s * (1.0 + gate * (1.0 - s)), gate_s


def hidden_units(x, weights, act, gate_f, up_f):
    values = hidden_values(x, weights)
    act[...], gate_f[...], up_f[...] = values
    return values[0]


def forward_pair_kernel(experts, width, expert, a, b, weights, kept, given, *units):
    n = a.shape[0]
    x = jnp.concatenate((a[:, :width], b[:, :width]))
    p = expert_weight(experts, expert, jnp.concatenate((a[:, width:], b[:, width:])))
    values = hidden_values(x, weights)
    out = p * weights.out(values[0])
    for i, value in enumerate((*values, jnp.broadcast_to(p, (2 * n, 128)))):
        units[i][...] = value[:n]
        units[i + 4][...] = value[n:]
    kept[...] = out[:n].astype(BF16)
    given[...] = out[n:].astype(BF16)


def forward_hidden_kernel(experts, width, expert, a, weights, act, gate_f, up_f, weight):
    weight[...] = jnp.broadcast_to(expert_weight(experts, expert, a[:, width:]), weight.shape)
    hidden_units(a[:, :width], weights, act, gate_f, up_f)


def forward_out_kernel(act, weight, weights, out):
    out[...] = (weight[:, :1] * weights.out(act[...])).astype(BF16)


def forward_full_kernel(experts, width, expert, a, weights, act, gate_f, up_f, weight, out):
    p = expert_weight(experts, expert, a[:, width:])
    weight[...] = jnp.broadcast_to(p, weight.shape)
    act_val = hidden_units(a[:, :width], weights, act, gate_f, up_f)
    out[...] = (p * weights.out(act_val)).astype(BF16)


def hidden_cots(cot, weight, gate_f, up_f, weights, gate_cot, up_cot, out_cot):
    out = (cot.astype(F32) * weight[:, :1]).astype(BF16)
    out_cot[...] = out
    act_cot = weights.act_cot(out)
    gate = (act_cot * gate_f[...]).astype(BF16)
    up = (act_cot * up_f[...]).astype(BF16)
    gate_cot[...], up_cot[...] = gate, up
    return gate, up


def backward_hidden_kernel(cot, weight, gate_f, up_f, weights, gate_cot, up_cot, out_cot):
    hidden_cots(cot[...], weight, gate_f, up_f, weights, gate_cot, up_cot, out_cot)


def backward_rows_kernel(gate, up, weights, out):
    out[...] = weights.row_cot(gate[...], up[...]).astype(BF16)


def backward_full_kernel(cot, weight, gate_f, up_f, weights, gate_cot, up_cot, out_cot, out):
    gate, up = hidden_cots(cot[...], weight, gate_f, up_f, weights, gate_cot, up_cot, out_cot)
    out[...] = weights.row_cot(gate, up).astype(BF16)


def chunk_kernel(over_left, chunks, counts, *refs):
    outs = len(counts) - 1
    joined = []
    for count in counts:
        joined.append(refs[:count])
        refs = refs[count:]
    results, held, sems = refs[:outs], refs[outs:-1], refs[-1]
    split = 0 if over_left else 1
    rest = [None if i == split else jnp.concatenate([r[...] for r in group]) for i, group in enumerate(joined)]
    if over_left:
        right = jnp.concatenate(rest[1:], axis=1)
    size = held[0].shape[split] // chunks
    copies = []
    for i in range(chunks):
        part = pl.ds(i * size, size)
        piece = jnp.concatenate([r[:, part] for r in joined[split]])
        value = tn(piece, right) if over_left else tn(rest[0], piece)
        for j in range(outs):
            width = value.shape[1] // outs
            at = (part, slice(None)) if over_left else (slice(None), part)
            held[j][at] = value[:, j * width : (j + 1) * width].astype(BF16)
            copy = pltpu.make_async_copy(held[j].at[at], results[j].at[(0, *at)], sems.at[i, j])
            copy.start()
            copies.append(copy)
    for copy in copies:
        copy.wait()


def gradients_by_chunks(left, rights, width, over_left, chunks=4):
    hidden = rights[0][0].shape[1]
    groups = [left, *rights]
    flat = [piece for group in groups for piece in group]
    return pl.pallas_call(
        functools.partial(chunk_kernel, over_left, chunks, [len(g) for g in groups]),
        in_specs=[WHOLE] * len(flat),
        out_specs=[ANY] * len(rights),
        out_shape=shaped(*[((1, width, hidden), BF16)] * len(rights)),
        scratch_shapes=[pltpu.VMEM((width, hidden), BF16)] * len(rights) + [pltpu.SemaphoreType.DMA((chunks, len(rights)))],
        compiler_params=params(16),
        cost_estimate=cost(10.0),
    )(*flat)


def gradient_kernel(width, counts, *refs):
    joined = []
    for count in counts:
        joined.append(jnp.concatenate([r[...] for r in refs[:count]]))
        refs = refs[count:]
    outs, total = refs[:-1], refs[-1]
    part = tn(joined[0][:, :width], jnp.concatenate(joined[1:], axis=1))

    def write(value):
        hidden = value.shape[1] // len(outs)
        for i, out in enumerate(outs):
            out[0] = value[:, i * hidden : (i + 1) * hidden].astype(BF16)

    if total.shape[0] == 8:
        write(part)
        return
    step = pl.program_id(0)

    @pl.when(step == 0)
    def _():
        total[...] = part

    @pl.when(step > 0)
    def _():
        total[...] += part

    @pl.when(step == pl.num_programs(0) - 1)
    def _():
        write(total[...])


def gradients(left, rights, width, steps):
    hidden = rights[0][0].shape[1]
    if steps == 1:
        over_left = width > hidden
        if max(width, hidden) % (4 * 128) == 0:
            return gradients_by_chunks(left, rights, width, over_left)
    groups = [left, *rights]
    flat = [piece for group in groups for piece in group]
    if steps == 1:
        specs = [WHOLE] * len(flat)
    else:
        specs = [pl.BlockSpec((a.shape[0] // steps, a.shape[1]), lambda i: (i, 0)) for a in flat]
    total = (8, 128) if steps == 1 else (width, len(rights) * hidden)
    return pl.pallas_call(
        functools.partial(gradient_kernel, width, [len(g) for g in groups]),
        grid=(steps,),
        in_specs=specs,
        out_specs=[pl.BlockSpec((1, width, hidden), lambda i: (0, 0, 0))] * len(rights),
        out_shape=shaped(*[((1, width, hidden), BF16)] * len(rights)),
        scratch_shapes=[pltpu.VMEM(total, F32)],
        compiler_params=params(24 if steps == 1 else 48),
        cost_estimate=cost(10.0),
    )(*flat)


def body(tokens, route, probs, cotangent, gate_weight, up_weight, down_weight):
    n_dp, n_ex = lax.axis_size("dp"), lax.axis_size("expert")
    experts = n_dp * n_ex // 2
    rows, width = tokens.shape
    hidden = gate_weight.shape[2]
    core, plane, line = permutes(n_dp, n_ex)
    expert = lax.shift_right_logical(lax.axis_index(AXES).astype(jnp.int32), 1).reshape(1, 1)
    expert, tokens = lax.optimization_barrier((expert, tokens))
    units = [(hidden, BF16), (hidden, F32), (hidden, F32), (128, F32)]
    cots = [(hidden, BF16), (hidden, BF16), (width, BF16)]
    wide = (1, width, BF16)

    def each(factor, arrays):
        return [(factor, *a) for a in arrays]

    own, cot = payload(tokens, cotangent, route, probs, experts)
    weights = (gate_weight, up_weight, down_weight)
    staged = n_ex * rows * 2 <= BLOCK
    if staged:
        weights = stage(*(after(w, own) for w in weights))
    for p in plane[:-1]:
        cot = join(cot, send(cot, p))
    row_lane = join(after(own, weights[0], cot), *[send(own, p) for p in line])
    cot = after(cot, row_lane)
    cot_lane = join(cot, *[send(cot, p) for p in line], length=10.0)
    for p in plane[:-1]:
        row_lane = join(row_lane, send(row_lane, p), blocks=n_ex)
    n = row_lane.shape[0]
    row_late = send(row_lane, plane[-1])
    row_other = send(row_lane, core)

    def forward(kernel, *args):
        return functools.partial(kernel, experts, width), n, [expert], *args

    f_early = over_rows(
        *forward(forward_pair_kernel, [(1, row_lane), (1, row_other)], weights, [wide] * 2 + each(1, units * 2))
    )
    kept, given, *f_early = f_early
    f_early = (f_early[:4], f_early[4:])
    cot_lane = after(cot_lane, kept)
    cot_late = send(cot_lane, plane[-1])
    cot_other = send(cot_lane, core)

    def halve(kept, received):
        return add(kept, received).astype(BF16)

    def with_units(f):
        return [(1, f[3]), (1, f[1]), (1, f[2])]

    row_late = after(row_late, cot_lane)
    row_late_other = send(row_late, core)
    f_own = over_rows(*forward(forward_hidden_kernel, [(1, row_late)], weights, each(1, units), 10.0))
    *f_other, o_given = over_rows(
        *forward(forward_full_kernel, [(1, row_late_other)], weights, each(1, units) + [wide], 10.0)
    )
    o_other = send(o_given, core)
    taken = [(1, f_own[0]), (1, after(f_own[3], f_other[0]))]
    (o_own,) = over_rows(forward_out_kernel, n, [], taken, weights, [wide], 10.0)
    taken = [(1, after(cot_lane, f_other[0]))] + with_units(f_early[0])
    *b_early, g_kept = over_rows(backward_full_kernel, n, [], taken, weights, each(1, cots) + [wide], 10.0)
    o_late = halve(o_own, after(o_other, g_kept))
    o_early_other = send(given, core)
    o_back = send(o_late, plane[-1])

    cot_late = after(cot_late, o_late)
    cot_late_other = send(cot_late, core)
    taken = [(1, cot_late)] + with_units(f_own)
    b_own = over_rows(backward_hidden_kernel, n, [], taken, weights, each(1, cots), 10.0)
    taken = [(1, after(cot_other, b_own[0]))] + with_units(f_early[1])
    *b_early_other, g_early = over_rows(backward_full_kernel, n, [], taken, weights, each(1, cots) + [wide], 10.0)
    taken = [(1, after(cot_late_other, g_early))] + with_units(f_other)
    *b_other, g_given = over_rows(backward_full_kernel, n, [], taken, weights, each(1, cots) + [wide], 10.0)
    g_other = send(g_given, core)
    taken = [(1, b_own[0]), (1, after(b_own[1], b_other[0]))]
    (g_own,) = over_rows(backward_rows_kernel, n, [], taken, weights, [wide], 10.0)
    g_late = halve(g_own, g_other)
    g_early_other = send(g_early, core)
    g_back = send(g_late, plane[-1])
    o_back = after(o_back, g_late)

    def line_sends(lane):
        rows = lane.shape[0] // n_ex
        return [lane[:rows]] + [send(lane[j * rows : (j + 1) * rows], p) for j, p in enumerate(line, 1)]

    steps = max(1, n // BLOCK)
    gate_cots, up_cots, out_cots = zip(b_early, b_early_other, b_own, b_other)

    parts = (g_kept, g_early_other, g_back)
    for p in reversed(plane[:-1]):
        g_lane, g_sent = split_sum(n_ex, *parts)
        parts = (g_lane, send(g_sent, p))
    lefts = [after(row_lane, g_sent), row_other, row_late, row_late_other]
    gate_grad, up_grad = gradients(lefts, [gate_cots, up_cots], width, steps)
    acts = [after(f_early[0][0], g_sent), f_early[1][0], f_own[0], f_other[0]]
    (down_grad,) = gradients(acts, [out_cots], hidden, steps)
    g_lane = add(parts[0], after(parts[1], gate_grad, down_grad)).astype(BF16)
    g_terms = line_sends(g_lane)
    o_terms = line_sends(add(kept, o_early_other, o_back).astype(BF16))
    parts = (join(after(o_terms[0], g_lane), length=20.0), *o_terms[1:])
    for p in reversed(plane[:-1]):
        lane = add(*parts).astype(BF16)
        half = lane.shape[0] // 2
        parts = (lane[:half], send(lane[half:], p))
    mixed, token_grad = last_sums(parts, g_terms)
    return mixed, token_grad, gate_grad, up_grad, down_grad


def solution(mesh):
    two, three = P(AXES, None), P(AXES, None, None)
    return jax.shard_map(
        body,
        mesh=mesh,
        in_specs=(two, two, two, two, three, three, three),
        out_specs=(two, two, three, three, three),
        check_vma=False,
    )
```

```python
import functools

import jax
import jax.numpy as jnp
from jax import lax
from jax.experimental import pallas as pl
from jax.experimental.pallas import tpu as pltpu
from jax.sharding import PartitionSpec as P

AXES = ("dp", "expert")
F32, BF16 = jnp.float32, jnp.bfloat16
BLOCK = 128


def permutes(n_dp, n_ex):
    def pairs(to):
        out = []
        for d in range(n_dp):
            for z in range(n_ex):
                e, y = to(d, z)
                out.append((d * n_ex + z, e * n_ex + y))
        return out

    def mixed(step, bits):
        def to(d, z):
            bit = step if d % 2 == 0 else bits - 1 - step
            return d ^ (2 << bit), z

        return pairs(to)

    bits = n_dp.bit_length() - 2
    core = pairs(lambda d, z: (d ^ 1, z))
    plane = [mixed(s, bits) for s in range(bits)]
    line = [pairs(lambda d, z, j=j: (d, z ^ j)) for j in reversed(range(1, n_ex))]
    return core, plane, line


def send(x, pairs):
    return lax.ppermute(x, AXES, pairs)


def after(x, *others):
    return lax.optimization_barrier((x, *others))[0]


def add(*terms):
    return functools.reduce(lambda a, b: a + b, [t.astype(F32) for t in terms])


def nt(left, right):
    return lax.dot_general(left, right, (((1,), (1,)), ((), ())), preferred_element_type=F32)


def tn(left, right):
    return lax.dot_general(left, right, (((0,), (0,)), ((), ())), preferred_element_type=F32)


def dot(left, right):
    return jnp.dot(left, right, preferred_element_type=F32)


def shaped(*arrays):
    return [jax.ShapeDtypeStruct(s, t) for s, t in arrays]


def params(mib):
    return pltpu.CompilerParams(vmem_limit_bytes=mib << 20)


def cost(microseconds):
    return pl.CostEstimate(flops=int(microseconds * 1.15e9), bytes_accessed=0, transcendentals=0)


WHOLE = pl.BlockSpec(memory_space=pltpu.VMEM)
ANY = pl.BlockSpec(memory_space=pltpu.HBM)


def payload_kernel(experts, tokens, cotangent, route_in, probs_in, out, cot, route, probs, sems):
    rows, width = tokens.shape
    copies = [
        pltpu.make_async_copy(a, b, sems.at[i])
        for i, (a, b) in enumerate(
            ((route_in, route), (probs_in, probs), (tokens, out.at[:, :width]), (cotangent, cot))
        )
    ]
    for copy in copies:
        copy.start()
    for copy in copies[:2]:
        copy.wait()
    extra = out.shape[1] - width
    column = lax.broadcasted_iota(jnp.int32, (extra, rows), 0)
    named, part = column, jnp.zeros_like(column)
    for _ in range(2):
        over = named >= experts
        named, part = jnp.where(over, named - experts, named), part + over.astype(jnp.int32)
    table = jnp.zeros((extra, rows), F32)
    for k in range(route.shape[0]):
        table = table + jnp.where(route[k : k + 1, :] == named, probs[k : k + 1, :], 0.0)
    high = table.astype(BF16).astype(F32)
    middle = (table - high).astype(BF16).astype(F32)
    low = table - high - middle
    table = jnp.where(part == 0, high, jnp.where(part == 1, middle, low))
    out[:, width:] = jnp.transpose(table).astype(BF16)
    for copy in copies[2:]:
        copy.wait()


def payload(tokens, cotangent, route, probs, experts):
    rows, width = tokens.shape
    extra = -(-3 * experts // 128) * 128
    return pl.pallas_call(
        functools.partial(payload_kernel, experts),
        in_specs=[ANY] * 4,
        out_specs=[WHOLE] * 2,
        out_shape=[pltpu.VMEM((rows, width + extra), BF16), pltpu.VMEM((rows, width), BF16)],
        scratch_shapes=[
            pltpu.VMEM(route.shape[::-1], jnp.int32),
            pltpu.VMEM(probs.shape[::-1], F32),
            pltpu.SemaphoreType.DMA((4,)),
        ],
        compiler_params=params(60),
    )(tokens, cotangent, route.T, probs.T)


def stage_kernel(gate, up, down, tall, wide, sems):
    copies = [
        pltpu.make_async_copy(a.at[0], b, sems.at[i])
        for i, (a, b) in enumerate(((gate, tall.at[0]), (up, tall.at[1]), (down, wide.at[2])))
    ]
    for copy in copies:
        copy.start()
    for i, copy in enumerate(copies):
        copy.wait()
        if i < 2:
            wide[i] = jnp.transpose(tall[i])
        else:
            tall[i] = jnp.transpose(wide[i])


def stage(gate, up, down):
    _, width, hidden = gate.shape
    return pl.pallas_call(
        stage_kernel,
        in_specs=[ANY] * 3,
        out_specs=[WHOLE] * 2,
        out_shape=[pltpu.VMEM((3, width, hidden), BF16), pltpu.VMEM((3, hidden, width), BF16)],
        scratch_shapes=[pltpu.SemaphoreType.DMA((3,))],
        compiler_params=params(52),
    )(gate, up, down)


class Weights:
    def __init__(self, refs):
        self.refs = refs
        self.staged = len(refs) == 2

    def hidden(self, x):
        if self.staged:
            return dot(x, self.refs[0][0]), dot(x, self.refs[0][1])
        return dot(x, self.refs[0][0]), dot(x, self.refs[1][0])

    def out(self, act):
        return dot(act, self.refs[1][2] if self.staged else self.refs[2][0])

    def act_cot(self, out_cot):
        return dot(out_cot, self.refs[0][2]) if self.staged else nt(out_cot, self.refs[2][0])

    def row_cot(self, gate, up):
        if self.staged:
            return dot(gate, self.refs[1][0]) + dot(up, self.refs[1][1])
        return nt(gate, self.refs[0][0]) + nt(up, self.refs[1][0])


def join_kernel(blocks, flip, *refs):
    at, out = 0, refs[-1]
    arrays = (refs[0], *refs[-2:0:-1]) if flip else refs[:-1]
    for i in range(blocks):
        for ref in arrays:
            size = ref.shape[0] // blocks
            out[at : at + size, :] = ref[i * size : (i + 1) * size, :]
            at += size


def join(*arrays, blocks=1, flip=False, length=0.0):
    rows = sum(a.shape[0] for a in arrays)
    return pl.pallas_call(
        functools.partial(join_kernel, blocks, flip),
        in_specs=[WHOLE] * len(arrays),
        out_specs=WHOLE,
        out_shape=pltpu.VMEM((rows, arrays[0].shape[1]), BF16),
        compiler_params=params(4),
        cost_estimate=cost(length),
    )(*arrays)


def split_sum_kernel(blocks, *refs):
    arrays, outs = refs[:-2], refs[-2:]
    half = outs[0].shape[0] // blocks
    for i in range(blocks):
        for j, out in enumerate(outs):
            rows = pl.ds((2 * i + j) * half, half)
            total = functools.reduce(lambda x, y: x + y, [r[rows, :].astype(F32) for r in arrays])
            out[i * half : (i + 1) * half, :] = total.astype(BF16)


def split_sum(blocks, *arrays):
    rows, width = arrays[0].shape
    return pl.pallas_call(
        functools.partial(split_sum_kernel, blocks),
        in_specs=[WHOLE] * len(arrays),
        out_specs=[WHOLE] * 2,
        out_shape=[pltpu.VMEM((rows // 2, width), BF16)] * 2,
        compiler_params=params(4),
        cost_estimate=cost(0.0),
    )(*arrays)


def grid_specs(block, arrays, whole):
    specs = [pl.BlockSpec((block * f, w), lambda i: (i, 0)) for f, w in arrays]
    return specs + [pl.BlockSpec(w.shape, lambda i: (0, 0, 0)) for w in whole]


def last_sums_kernel(counts, *refs):
    taken, results, held, sems = refs[: sum(counts)], refs[-5:-3], refs[-3:-1], refs[-1]
    copies = []
    for i, count in enumerate(counts):
        total = functools.reduce(lambda x, y: x + y, [r[...].astype(F32) for r in taken[:count]])
        taken = taken[count:]
        held[i][...] = total.astype(BF16)
        copies.append(pltpu.make_async_copy(held[i], results[i], sems.at[i]))
        copies[i].start()
    for copy in copies:
        copy.wait()


def last_sums(*groups):
    shape = groups[0][0].shape
    return pl.pallas_call(
        functools.partial(last_sums_kernel, [len(g) for g in groups]),
        in_specs=[WHOLE] * sum(len(g) for g in groups),
        out_specs=[ANY] * len(groups),
        out_shape=shaped(*[(shape, BF16)] * len(groups)),
        scratch_shapes=[pltpu.VMEM(shape, BF16)] * len(groups) + [pltpu.SemaphoreType.DMA((len(groups),))],
        compiler_params=params(4),
        cost_estimate=cost(0.0),
    )(*[a for g in groups for a in g])


def over_rows(kernel, n, scalars, taken, weights, given, length=0.0):
    block = min(n, BLOCK)
    if block == n:
        call = dict(in_specs=[WHOLE] * (len(taken) + len(weights)), out_specs=[WHOLE] * len(given))
    else:
        call = dict(
            grid=(n // block,),
            in_specs=grid_specs(block, [(f, a.shape[1]) for f, a in taken], weights),
            out_specs=grid_specs(block, [(f, w) for f, w, _ in given], []),
        )
    call["in_specs"] = [pl.BlockSpec(memory_space=pltpu.SMEM)] * len(scalars) + call["in_specs"]
    first = len(scalars) + len(taken)

    def run(*refs):
        kernel(*refs[:first], Weights(refs[first : first + len(weights)]), *refs[first + len(weights) :])

    return pl.pallas_call(
        run,
        out_shape=shaped(*[((f * n, w), t) for f, w, t in given]),
        compiler_params=params(12 if block == n else 40),
        cost_estimate=cost(length),
        **call,
    )(*scalars, *[a for _, a in taken], *weights)


def expert_weight(experts, expert, table):
    column = lax.broadcasted_iota(jnp.int32, table.shape, 1)
    mine = expert[0, 0]
    mine = (column == mine) | (column == mine + experts) | (column == mine + 2 * experts)
    return jnp.sum(jnp.where(mine, table.astype(F32), 0.0), axis=1, keepdims=True)


def hidden_values(x, weights):
    gate, up = weights.hidden(x)
    s = jax.nn.sigmoid(gate)
    gate_s = gate * s
    return (gate_s * up).astype(BF16), up * s * (1.0 + gate * (1.0 - s)), gate_s


def hidden_units(x, weights, act, gate_f, up_f):
    values = hidden_values(x, weights)
    act[...], gate_f[...], up_f[...] = values
    return values[0]


def forward_hidden_kernel(experts, width, expert, a, weights, act, gate_f, up_f, weight):
    weight[...] = jnp.broadcast_to(expert_weight(experts, expert, a[:, width:]), weight.shape)
    hidden_units(a[:, :width], weights, act, gate_f, up_f)


def forward_out_kernel(act, weight, weights, out):
    out[...] = (weight[:, :1] * weights.out(act[...])).astype(BF16)


def forward_full_kernel(experts, width, expert, a, weights, act, gate_f, up_f, weight, out):
    p = expert_weight(experts, expert, a[:, width:])
    weight[...] = jnp.broadcast_to(p, weight.shape)
    act_val = hidden_units(a[:, :width], weights, act, gate_f, up_f)
    out[...] = (p * weights.out(act_val)).astype(BF16)


def hidden_cots(cot, weight, gate_f, up_f, weights, gate_cot, up_cot, out_cot):
    out = (cot.astype(F32) * weight[:, :1]).astype(BF16)
    out_cot[...] = out
    act_cot = weights.act_cot(out)
    gate = (act_cot * gate_f[...]).astype(BF16)
    up = (act_cot * up_f[...]).astype(BF16)
    gate_cot[...], up_cot[...] = gate, up
    return gate, up


def backward_hidden_kernel(cot, weight, gate_f, up_f, weights, gate_cot, up_cot, out_cot):
    hidden_cots(cot[...], weight, gate_f, up_f, weights, gate_cot, up_cot, out_cot)


def backward_rows_kernel(gate, up, weights, out):
    out[...] = weights.row_cot(gate[...], up[...]).astype(BF16)


def backward_full_kernel(cot, weight, gate_f, up_f, weights, gate_cot, up_cot, out_cot, out):
    gate, up = hidden_cots(cot[...], weight, gate_f, up_f, weights, gate_cot, up_cot, out_cot)
    out[...] = weights.row_cot(gate, up).astype(BF16)


def chunk_kernel(over_left, chunks, counts, *refs):
    outs = len(counts) - 1
    joined = []
    for count in counts:
        joined.append(refs[:count])
        refs = refs[count:]
    results, held, sems = refs[:outs], refs[outs:-1], refs[-1]
    split = 0 if over_left else 1
    rest = [None if i == split else jnp.concatenate([r[...] for r in group]) for i, group in enumerate(joined)]
    if over_left:
        right = jnp.concatenate(rest[1:], axis=1)
    size = held[0].shape[split] // chunks
    copies = []
    for i in range(chunks):
        part = pl.ds(i * size, size)
        piece = jnp.concatenate([r[:, part] for r in joined[split]])
        value = tn(piece, right) if over_left else tn(rest[0], piece)
        for j in range(outs):
            width = value.shape[1] // outs
            at = (part, slice(None)) if over_left else (slice(None), part)
            held[j][at] = value[:, j * width : (j + 1) * width].astype(BF16)
            copy = pltpu.make_async_copy(held[j].at[at], results[j].at[(0, *at)], sems.at[i, j])
            copy.start()
            copies.append(copy)
    for copy in copies:
        copy.wait()


def gradients_by_chunks(left, rights, width, over_left, chunks=4):
    hidden = rights[0][0].shape[1]
    groups = [left, *rights]
    flat = [piece for group in groups for piece in group]
    return pl.pallas_call(
        functools.partial(chunk_kernel, over_left, chunks, [len(g) for g in groups]),
        in_specs=[WHOLE] * len(flat),
        out_specs=[ANY] * len(rights),
        out_shape=shaped(*[((1, width, hidden), BF16)] * len(rights)),
        scratch_shapes=[pltpu.VMEM((width, hidden), BF16)] * len(rights) + [pltpu.SemaphoreType.DMA((chunks, len(rights)))],
        compiler_params=params(16),
        cost_estimate=cost(10.0),
    )(*flat)


def gradient_kernel(width, counts, *refs):
    joined = []
    for count in counts:
        joined.append(jnp.concatenate([r[...] for r in refs[:count]]))
        refs = refs[count:]
    outs, total = refs[:-1], refs[-1]
    part = tn(joined[0][:, :width], jnp.concatenate(joined[1:], axis=1))

    def write(value):
        hidden = value.shape[1] // len(outs)
        for i, out in enumerate(outs):
            out[0] = value[:, i * hidden : (i + 1) * hidden].astype(BF16)

    if total.shape[0] == 8:
        write(part)
        return
    step = pl.program_id(0)

    @pl.when(step == 0)
    def _():
        total[...] = part

    @pl.when(step > 0)
    def _():
        total[...] += part

    @pl.when(step == pl.num_programs(0) - 1)
    def _():
        write(total[...])


def gradients(left, rights, width, steps):
    hidden = rights[0][0].shape[1]
    if steps == 1:
        over_left = width > hidden
        if max(width, hidden) % (4 * 128) == 0:
            return gradients_by_chunks(left, rights, width, over_left)
    groups = [left, *rights]
    flat = [piece for group in groups for piece in group]
    if steps == 1:
        specs = [WHOLE] * len(flat)
    else:
        specs = [pl.BlockSpec((a.shape[0] // steps, a.shape[1]), lambda i: (i, 0)) for a in flat]
    total = (8, 128) if steps == 1 else (width, len(rights) * hidden)
    return pl.pallas_call(
        functools.partial(gradient_kernel, width, [len(g) for g in groups]),
        grid=(steps,),
        in_specs=specs,
        out_specs=[pl.BlockSpec((1, width, hidden), lambda i: (0, 0, 0))] * len(rights),
        out_shape=shaped(*[((1, width, hidden), BF16)] * len(rights)),
        scratch_shapes=[pltpu.VMEM(total, F32)],
        compiler_params=params(24 if steps == 1 else 48),
        cost_estimate=cost(10.0),
    )(*flat)


def body(tokens, route, probs, cotangent, gate_weight, up_weight, down_weight):
    n_dp, n_ex = lax.axis_size("dp"), lax.axis_size("expert")
    experts = n_dp * n_ex // 2
    rows, width = tokens.shape
    hidden = gate_weight.shape[2]
    core, plane, line = permutes(n_dp, n_ex)
    expert = lax.shift_right_logical(lax.axis_index(AXES).astype(jnp.int32), 1).reshape(1, 1)
    expert, tokens = lax.optimization_barrier((expert, tokens))
    units = [(hidden, BF16), (hidden, F32), (hidden, F32), (128, F32)]
    cots = [(hidden, BF16), (hidden, BF16), (width, BF16)]
    wide = (1, width, BF16)

    def each(factor, arrays):
        return [(factor, *a) for a in arrays]

    own, cot = payload(tokens, cotangent, route, probs, experts)
    weights = (gate_weight, up_weight, down_weight)
    staged = n_ex * rows * 2 <= BLOCK
    if staged:
        weights = stage(*(after(w, own) for w in weights))
    for p in plane[:-1]:
        cot = join(cot, send(cot, p))
    row_lane = join(after(own, weights[0], cot), *[send(own, p) for p in line[::-1]], flip=True)
    cot = after(cot, row_lane)
    cot_lane = join(cot, *[send(cot, p) for p in line], length=10.0)
    for p in plane[:-1]:
        row_lane = join(row_lane, send(row_lane, p), blocks=n_ex)
    n = row_lane.shape[0]
    row_late = send(row_lane, plane[-1])
    row_other = send(row_lane, core)

    def forward(kernel, *args):
        return functools.partial(kernel, experts, width), n, [expert], *args

    cot_late = send(cot_lane, plane[-1])
    cot_other = send(cot_lane, core)

    def halve(kept, received):
        return add(kept, received).astype(BF16)

    def with_units(f):
        return [(1, f[3]), (1, f[1]), (1, f[2])]

    row_late = after(row_late, cot_lane)
    row_late_other = send(row_late, core)
    f_own = over_rows(*forward(forward_hidden_kernel, [(1, row_late)], weights, each(1, units), 10.0))
    full = weights, each(1, units) + [wide], 10.0
    *f_early_own, kept = over_rows(*forward(forward_full_kernel, [(1, after(row_lane, f_own[0]))], *full))
    row_late_other_in = after(row_late_other, kept)
    *f_other, o_given = over_rows(*forward(forward_full_kernel, [(1, row_late_other_in)], *full))
    o_other = send(o_given, core)
    *f_early_other, given = over_rows(*forward(forward_full_kernel, [(1, after(row_other, f_other[0]))], *full))
    taken = [(1, f_own[0]), (1, after(f_own[3], given))]
    (o_own,) = over_rows(forward_out_kernel, n, [], taken, weights, [wide])
    o_late = halve(o_own, o_other)
    o_early_other = send(given, core)
    o_back = send(o_late, plane[-1])

    cot_late = after(cot_late, o_late)
    cot_late_other = send(cot_late, core)
    taken = [(1, cot_late)] + with_units(f_own)
    b_own = over_rows(backward_hidden_kernel, n, [], taken, weights, each(1, cots), 10.0)
    full = weights, each(1, cots) + [wide], 10.0
    taken = [(1, after(cot_lane, b_own[0]))] + with_units(f_early_own)
    *b_early, g_kept = over_rows(backward_full_kernel, n, [], taken, *full)
    taken = [(1, after(cot_late_other, g_kept))] + with_units(f_other)
    *b_other, g_given = over_rows(backward_full_kernel, n, [], taken, *full)
    g_other = send(g_given, core)
    taken = [(1, after(cot_other, b_other[0]))] + with_units(f_early_other)
    *b_early_other, g_early = over_rows(backward_full_kernel, n, [], taken, *full)
    taken = [(1, b_own[0]), (1, after(b_own[1], g_early))]
    (g_own,) = over_rows(backward_rows_kernel, n, [], taken, weights, [wide])
    g_late = halve(g_own, g_other)
    g_early_other = send(after(g_early, g_late), core)
    g_back = send(g_late, plane[-1])
    o_back = after(o_back, g_late)

    def line_sends(lane):
        rows = lane.shape[0] // n_ex
        return [lane[:rows]] + [send(lane[j * rows : (j + 1) * rows], p) for j, p in enumerate(line, 1)]

    steps = max(1, n // BLOCK)
    gate_cots, up_cots, out_cots = zip(b_early, b_early_other, b_own, b_other)

    g_sent = g_late
    parts = (g_kept, g_early_other, g_back)
    for p in reversed(plane[:-1]):
        g_lane, g_sent = split_sum(n_ex, *parts)
        parts = (g_lane, send(g_sent, p))
    lefts = [after(row_lane, g_sent), row_other, row_late, row_late_other]
    gate_grad, up_grad = gradients(lefts, [gate_cots, up_cots], width, steps)
    acts = [after(f_early_own[0], g_sent), f_early_other[0], f_own[0], f_other[0]]
    (down_grad,) = gradients(acts, [out_cots], hidden, steps)
    g_lane = add(parts[0], after(parts[1], gate_grad, down_grad)).astype(BF16)
    g_terms = line_sends(g_lane)
    o_terms = line_sends(add(kept, o_early_other, o_back).astype(BF16))
    parts = (join(after(o_terms[0], g_lane), length=20.0), *o_terms[1:])
    for p in reversed(plane[:-1]):
        lane = add(*parts).astype(BF16)
        half = lane.shape[0] // 2
        parts = (lane[:half], send(lane[half:], p))
    mixed, token_grad = last_sums(parts, g_terms)
    return mixed, token_grad, gate_grad, up_grad, down_grad


def solution(mesh):
    two, three = P(AXES, None), P(AXES, None, None)
    return jax.shard_map(
        body,
        mesh=mesh,
        in_specs=(two, two, two, two, three, three, three),
        out_specs=(two, two, three, three, three),
        check_vma=False,
    )
```

```python
import functools

import jax
import jax.numpy as jnp
from jax import lax
from jax.experimental import pallas as pl
from jax.experimental.pallas import tpu as pltpu
from jax.sharding import PartitionSpec as P

AXES = ("dp", "expert")
F32, BF16 = jnp.float32, jnp.bfloat16
BLOCK = 128


def permutes(n_dp, n_ex):
    def pairs(to):
        out = []
        for d in range(n_dp):
            for z in range(n_ex):
                e, y = to(d, z)
                out.append((d * n_ex + z, e * n_ex + y))
        return out

    def mixed(step, bits):
        def to(d, z):
            bit = step if d % 2 == 0 else bits - 1 - step
            return d ^ (2 << bit), z

        return pairs(to)

    bits = n_dp.bit_length() - 2
    core = pairs(lambda d, z: (d ^ 1, z))
    plane = [mixed(s, bits) for s in range(bits)]
    line = [pairs(lambda d, z, j=j: (d, z ^ j)) for j in reversed(range(1, n_ex))]
    return core, plane, line


def send(x, pairs):
    return lax.ppermute(x, AXES, pairs)


def after(x, *others):
    return lax.optimization_barrier((x, *others))[0]


def add(*terms):
    return functools.reduce(lambda a, b: a + b, [t.astype(F32) for t in terms])


def nt(left, right):
    return lax.dot_general(left, right, (((1,), (1,)), ((), ())), preferred_element_type=F32)


def tn(left, right):
    return lax.dot_general(left, right, (((0,), (0,)), ((), ())), preferred_element_type=F32)


def dot(left, right):
    return jnp.dot(left, right, preferred_element_type=F32)


def shaped(*arrays):
    return [jax.ShapeDtypeStruct(s, t) for s, t in arrays]


def params(mib):
    return pltpu.CompilerParams(vmem_limit_bytes=mib << 20)


def cost(microseconds):
    return pl.CostEstimate(flops=int(microseconds * 1.15e9), bytes_accessed=0, transcendentals=0)


WHOLE = pl.BlockSpec(memory_space=pltpu.VMEM)
ANY = pl.BlockSpec(memory_space=pltpu.HBM)


def payload_kernel(experts, tokens, cotangent, route_in, probs_in, out, cot, route, probs, sems):
    rows, width = tokens.shape
    copies = [
        pltpu.make_async_copy(a, b, sems.at[i])
        for i, (a, b) in enumerate(
            ((route_in, route), (probs_in, probs), (tokens, out.at[:, :width]), (cotangent, cot))
        )
    ]
    for copy in copies:
        copy.start()
    for copy in copies[:2]:
        copy.wait()
    extra = out.shape[1] - width
    column = lax.broadcasted_iota(jnp.int32, (extra, rows), 0)
    named, part = column, jnp.zeros_like(column)
    for _ in range(2):
        over = named >= experts
        named, part = jnp.where(over, named - experts, named), part + over.astype(jnp.int32)
    table = jnp.zeros((extra, rows), F32)
    for k in range(route.shape[0]):
        table = table + jnp.where(route[k : k + 1, :] == named, probs[k : k + 1, :], 0.0)
    high = table.astype(BF16).astype(F32)
    middle = (table - high).astype(BF16).astype(F32)
    low = table - high - middle
    table = jnp.where(part == 0, high, jnp.where(part == 1, middle, low))
    out[:, width:] = jnp.transpose(table).astype(BF16)
    for copy in copies[2:]:
        copy.wait()


def payload(tokens, cotangent, route, probs, experts):
    rows, width = tokens.shape
    extra = -(-3 * experts // 128) * 128
    return pl.pallas_call(
        functools.partial(payload_kernel, experts),
        in_specs=[ANY] * 4,
        out_specs=[WHOLE] * 2,
        out_shape=[pltpu.VMEM((rows, width + extra), BF16), pltpu.VMEM((rows, width), BF16)],
        scratch_shapes=[
            pltpu.VMEM(route.shape[::-1], jnp.int32),
            pltpu.VMEM(probs.shape[::-1], F32),
            pltpu.SemaphoreType.DMA((4,)),
        ],
        compiler_params=params(60),
    )(tokens, cotangent, route.T, probs.T)


def stage_kernel(gate, up, down, tall, wide, sems):
    copies = [
        pltpu.make_async_copy(a.at[0], b, sems.at[i])
        for i, (a, b) in enumerate(((gate, tall.at[0]), (up, tall.at[1]), (down, wide.at[2])))
    ]
    for copy in copies:
        copy.start()
    for i, copy in enumerate(copies):
        copy.wait()
        if i < 2:
            wide[i] = jnp.transpose(tall[i])
        else:
            tall[i] = jnp.transpose(wide[i])


def stage(gate, up, down):
    _, width, hidden = gate.shape
    return pl.pallas_call(
        stage_kernel,
        in_specs=[ANY] * 3,
        out_specs=[WHOLE] * 2,
        out_shape=[pltpu.VMEM((3, width, hidden), BF16), pltpu.VMEM((3, hidden, width), BF16)],
        scratch_shapes=[pltpu.SemaphoreType.DMA((3,))],
        compiler_params=params(52),
    )(gate, up, down)


class Weights:
    def __init__(self, refs):
        self.refs = refs
        self.staged = len(refs) == 2

    def hidden(self, x):
        if self.staged:
            return dot(x, self.refs[0][0]), dot(x, self.refs[0][1])
        return dot(x, self.refs[0][0]), dot(x, self.refs[1][0])

    def out(self, act):
        return dot(act, self.refs[1][2] if self.staged else self.refs[2][0])

    def act_cot(self, out_cot):
        return dot(out_cot, self.refs[0][2]) if self.staged else nt(out_cot, self.refs[2][0])

    def row_cot(self, gate, up):
        if self.staged:
            return dot(gate, self.refs[1][0]) + dot(up, self.refs[1][1])
        return nt(gate, self.refs[0][0]) + nt(up, self.refs[1][0])


def join_kernel(blocks, flip, *refs):
    at, out = 0, refs[-1]
    arrays = (refs[0], *refs[-2:0:-1]) if flip else refs[:-1]
    for i in range(blocks):
        for ref in arrays:
            size = ref.shape[0] // blocks
            out[at : at + size, :] = ref[i * size : (i + 1) * size, :]
            at += size


def join(*arrays, blocks=1, flip=False, length=0.0):
    rows = sum(a.shape[0] for a in arrays)
    return pl.pallas_call(
        functools.partial(join_kernel, blocks, flip),
        in_specs=[WHOLE] * len(arrays),
        out_specs=WHOLE,
        out_shape=pltpu.VMEM((rows, arrays[0].shape[1]), BF16),
        compiler_params=params(4),
        cost_estimate=cost(length),
    )(*arrays)


def split_sum_kernel(blocks, *refs):
    arrays, outs = refs[:-2], refs[-2:]
    half = outs[0].shape[0] // blocks
    for i in range(blocks):
        for j, out in enumerate(outs):
            rows = pl.ds((2 * i + j) * half, half)
            total = functools.reduce(lambda x, y: x + y, [r[rows, :].astype(F32) for r in arrays])
            out[i * half : (i + 1) * half, :] = total.astype(BF16)


def split_sum(blocks, *arrays):
    rows, width = arrays[0].shape
    return pl.pallas_call(
        functools.partial(split_sum_kernel, blocks),
        in_specs=[WHOLE] * len(arrays),
        out_specs=[WHOLE] * 2,
        out_shape=[pltpu.VMEM((rows // 2, width), BF16)] * 2,
        compiler_params=params(4),
        cost_estimate=cost(0.0),
    )(*arrays)


def grid_specs(block, arrays, whole):
    specs = [pl.BlockSpec((block * f, w), lambda i: (i, 0)) for f, w in arrays]
    return specs + [pl.BlockSpec(w.shape, lambda i: (0, 0, 0)) for w in whole]


def sum_kernel(*refs):
    refs[-1][...] = functools.reduce(lambda x, y: x + y, [r[...].astype(F32) for r in refs[:-1]]).astype(BF16)


def summed(*arrays, length=0.0):
    return pl.pallas_call(
        sum_kernel,
        in_specs=[WHOLE] * len(arrays),
        out_specs=WHOLE,
        out_shape=pltpu.VMEM(arrays[0].shape, BF16),
        compiler_params=params(4),
        cost_estimate=cost(length),
    )(*arrays)


def last_sums_kernel(counts, *refs):
    taken, results, held, sems = refs[: sum(counts)], refs[-5:-3], refs[-3:-1], refs[-1]
    copies = []
    for i, count in enumerate(counts):
        total = functools.reduce(lambda x, y: x + y, [r[...].astype(F32) for r in taken[:count]])
        taken = taken[count:]
        held[i][...] = total.astype(BF16)
        copies.append(pltpu.make_async_copy(held[i], results[i], sems.at[i]))
        copies[i].start()
    for copy in copies:
        copy.wait()


def last_sums(*groups):
    shape = groups[0][0].shape
    return pl.pallas_call(
        functools.partial(last_sums_kernel, [len(g) for g in groups]),
        in_specs=[WHOLE] * sum(len(g) for g in groups),
        out_specs=[ANY] * len(groups),
        out_shape=shaped(*[(shape, BF16)] * len(groups)),
        scratch_shapes=[pltpu.VMEM(shape, BF16)] * len(groups) + [pltpu.SemaphoreType.DMA((len(groups),))],
        compiler_params=params(4),
        cost_estimate=cost(0.0),
    )(*[a for g in groups for a in g])


def over_rows(kernel, n, scalars, taken, weights, given, length=0.0):
    block = min(n, BLOCK)
    if block == n:
        call = dict(in_specs=[WHOLE] * (len(taken) + len(weights)), out_specs=[WHOLE] * len(given))
    else:
        call = dict(
            grid=(n // block,),
            in_specs=grid_specs(block, [(f, a.shape[1]) for f, a in taken], weights),
            out_specs=grid_specs(block, [(f, w) for f, w, _ in given], []),
        )
    call["in_specs"] = [pl.BlockSpec(memory_space=pltpu.SMEM)] * len(scalars) + call["in_specs"]
    first = len(scalars) + len(taken)

    def run(*refs):
        kernel(*refs[:first], Weights(refs[first : first + len(weights)]), *refs[first + len(weights) :])

    return pl.pallas_call(
        run,
        out_shape=shaped(*[((f * n, w), t) for f, w, t in given]),
        compiler_params=params(12 if block == n else 40),
        cost_estimate=cost(length),
        **call,
    )(*scalars, *[a for _, a in taken], *weights)


def expert_weight(experts, expert, table):
    column = lax.broadcasted_iota(jnp.int32, table.shape, 1)
    mine = expert[0, 0]
    mine = (column == mine) | (column == mine + experts) | (column == mine + 2 * experts)
    return jnp.sum(jnp.where(mine, table.astype(F32), 0.0), axis=1, keepdims=True)


def hidden_values(x, weights):
    gate, up = weights.hidden(x)
    s = jax.nn.sigmoid(gate)
    gate_s = gate * s
    return (gate_s * up).astype(BF16), up * s * (1.0 + gate * (1.0 - s)), gate_s


def hidden_units(x, weights, act, gate_f, up_f):
    values = hidden_values(x, weights)
    act[...], gate_f[...], up_f[...] = values
    return values[0]


def forward_hidden_kernel(experts, width, expert, a, weights, act, gate_f, up_f, weight):
    weight[...] = jnp.broadcast_to(expert_weight(experts, expert, a[:, width:]), weight.shape)
    hidden_units(a[:, :width], weights, act, gate_f, up_f)


def forward_out_kernel(act, weight, weights, out):
    out[...] = (weight[:, :1] * weights.out(act[...])).astype(out.dtype)


def forward_full_kernel(experts, width, expert, a, weights, act, gate_f, up_f, weight, out):
    p = expert_weight(experts, expert, a[:, width:])
    weight[...] = jnp.broadcast_to(p, weight.shape)
    act_val = hidden_units(a[:, :width], weights, act, gate_f, up_f)
    out[...] = (p * weights.out(act_val)).astype(out.dtype)


def hidden_cots(cot, weight, gate_f, up_f, weights, gate_cot, up_cot, out_cot):
    out = (cot.astype(F32) * weight[:, :1]).astype(BF16)
    out_cot[...] = out
    act_cot = weights.act_cot(out)
    gate = (act_cot * gate_f[...]).astype(BF16)
    up = (act_cot * up_f[...]).astype(BF16)
    gate_cot[...], up_cot[...] = gate, up
    return gate, up


def backward_hidden_kernel(cot, weight, gate_f, up_f, weights, gate_cot, up_cot, out_cot):
    hidden_cots(cot[...], weight, gate_f, up_f, weights, gate_cot, up_cot, out_cot)


def backward_rows_kernel(gate, up, weights, out):
    out[...] = weights.row_cot(gate[...], up[...]).astype(out.dtype)


def backward_full_kernel(cot, weight, gate_f, up_f, weights, gate_cot, up_cot, out_cot, out):
    gate, up = hidden_cots(cot[...], weight, gate_f, up_f, weights, gate_cot, up_cot, out_cot)
    out[...] = weights.row_cot(gate, up).astype(out.dtype)


def chunk_kernel(over_left, chunks, counts, *refs):
    outs = len(counts) - 1
    joined = []
    for count in counts:
        joined.append(refs[:count])
        refs = refs[count:]
    results, held, sems = refs[:outs], refs[outs:-1], refs[-1]
    split = 0 if over_left else 1
    rest = [None if i == split else jnp.concatenate([r[...] for r in group]) for i, group in enumerate(joined)]
    if over_left:
        right = jnp.concatenate(rest[1:], axis=1)
    size = held[0].shape[split] // chunks
    copies = []
    for i in range(chunks):
        part = pl.ds(i * size, size)
        piece = jnp.concatenate([r[:, part] for r in joined[split]])
        value = tn(piece, right) if over_left else tn(rest[0], piece)
        for j in range(outs):
            width = value.shape[1] // outs
            at = (part, slice(None)) if over_left else (slice(None), part)
            held[j][at] = value[:, j * width : (j + 1) * width].astype(BF16)
            copy = pltpu.make_async_copy(held[j].at[at], results[j].at[(0, *at)], sems.at[i, j])
            copy.start()
            copies.append(copy)
    for copy in copies:
        copy.wait()


def gradients_by_chunks(left, rights, width, over_left, chunks=4):
    hidden = rights[0][0].shape[1]
    groups = [left, *rights]
    flat = [piece for group in groups for piece in group]
    return pl.pallas_call(
        functools.partial(chunk_kernel, over_left, chunks, [len(g) for g in groups]),
        in_specs=[WHOLE] * len(flat),
        out_specs=[ANY] * len(rights),
        out_shape=shaped(*[((1, width, hidden), BF16)] * len(rights)),
        scratch_shapes=[pltpu.VMEM((width, hidden), BF16)] * len(rights) + [pltpu.SemaphoreType.DMA((chunks, len(rights)))],
        compiler_params=params(16),
        cost_estimate=cost(10.0),
    )(*flat)


def gradient_kernel(width, counts, *refs):
    joined = []
    for count in counts:
        joined.append(jnp.concatenate([r[...] for r in refs[:count]]))
        refs = refs[count:]
    outs, total = refs[:-1], refs[-1]
    part = tn(joined[0][:, :width], jnp.concatenate(joined[1:], axis=1))

    def write(value):
        hidden = value.shape[1] // len(outs)
        for i, out in enumerate(outs):
            out[0] = value[:, i * hidden : (i + 1) * hidden].astype(BF16)

    if total.shape[0] == 8:
        write(part)
        return
    step = pl.program_id(0)

    @pl.when(step == 0)
    def _():
        total[...] = part

    @pl.when(step > 0)
    def _():
        total[...] += part

    @pl.when(step == pl.num_programs(0) - 1)
    def _():
        write(total[...])


def gradients(left, rights, width, steps):
    hidden = rights[0][0].shape[1]
    if steps == 1:
        over_left = width > hidden
        if max(width, hidden) % (4 * 128) == 0:
            return gradients_by_chunks(left, rights, width, over_left)
    groups = [left, *rights]
    flat = [piece for group in groups for piece in group]
    if steps == 1:
        specs = [WHOLE] * len(flat)
    else:
        specs = [pl.BlockSpec((a.shape[0] // steps, a.shape[1]), lambda i: (i, 0)) for a in flat]
    total = (8, 128) if steps == 1 else (width, len(rights) * hidden)
    return pl.pallas_call(
        functools.partial(gradient_kernel, width, [len(g) for g in groups]),
        grid=(steps,),
        in_specs=specs,
        out_specs=[pl.BlockSpec((1, width, hidden), lambda i: (0, 0, 0))] * len(rights),
        out_shape=shaped(*[((1, width, hidden), BF16)] * len(rights)),
        scratch_shapes=[pltpu.VMEM(total, F32)],
        compiler_params=params(24 if steps == 1 else 48),
        cost_estimate=cost(10.0),
    )(*flat)


def body(tokens, route, probs, cotangent, gate_weight, up_weight, down_weight):
    n_dp, n_ex = lax.axis_size("dp"), lax.axis_size("expert")
    experts = n_dp * n_ex // 2
    rows, width = tokens.shape
    hidden = gate_weight.shape[2]
    core, plane, line = permutes(n_dp, n_ex)
    expert = lax.shift_right_logical(lax.axis_index(AXES).astype(jnp.int32), 1).reshape(1, 1)
    expert, tokens = lax.optimization_barrier((expert, tokens))
    units = [(hidden, BF16), (hidden, F32), (hidden, F32), (128, F32)]
    cots = [(hidden, BF16), (hidden, BF16), (width, BF16)]
    wide, wide_kept = (1, width, BF16), (1, width, F32)

    def each(factor, arrays):
        return [(factor, *a) for a in arrays]

    own, cot = payload(tokens, cotangent, route, probs, experts)
    weights = (gate_weight, up_weight, down_weight)
    staged = n_ex * rows * 2 <= BLOCK
    if staged:
        weights = stage(*(after(w, own) for w in weights))
    for p in plane[:-1]:
        cot = join(cot, send(cot, p))
    row_lane = join(after(own, weights[0], cot), *[send(own, p) for p in line[::-1]], flip=True)
    cot = after(cot, row_lane)
    cot_lane = join(cot, *[send(cot, p) for p in line], length=10.0)
    for p in plane[:-1]:
        row_lane = join(row_lane, send(row_lane, p), blocks=n_ex)
    n = row_lane.shape[0]
    row_late = send(row_lane, plane[-1])
    row_other = send(row_lane, core)

    def forward(kernel, *args):
        return functools.partial(kernel, experts, width), n, [expert], *args

    cot_late = send(cot_lane, plane[-1])
    cot_other = send(cot_lane, core)

    def halve(kept, received):
        return add(kept, received).astype(BF16)

    def with_units(f):
        return [(1, f[3]), (1, f[1]), (1, f[2])]

    row_late = after(row_late, cot_lane)
    row_late_other = send(row_late, core)
    f_own = over_rows(*forward(forward_hidden_kernel, [(1, row_late)], weights, each(1, units), 10.0))
    full = weights, each(1, units) + [wide], 10.0
    *f_early_own, kept = over_rows(
        *forward(forward_full_kernel, [(1, after(row_lane, f_own[0]))], weights, each(1, units) + [wide_kept], 10.0)
    )
    row_late_other_in = after(row_late_other, kept)
    *f_other, o_given = over_rows(*forward(forward_full_kernel, [(1, row_late_other_in)], *full))
    o_other = send(o_given, core)
    *f_early_other, given = over_rows(*forward(forward_full_kernel, [(1, after(row_other, f_other[0]))], *full))
    taken = [(1, f_own[0]), (1, after(f_own[3], given))]
    (o_own,) = over_rows(forward_out_kernel, n, [], taken, weights, [wide_kept])
    o_late = halve(o_own, o_other)
    o_early_other = send(given, core)
    o_back = send(o_late, plane[-1])

    cot_late = after(cot_late, o_late)
    cot_late_other = send(cot_late, core)
    taken = [(1, cot_late)] + with_units(f_own)
    b_own = over_rows(backward_hidden_kernel, n, [], taken, weights, each(1, cots), 10.0)
    full = weights, each(1, cots) + [wide], 10.0
    taken = [(1, after(cot_lane, b_own[0]))] + with_units(f_early_own)
    *b_early, g_kept = over_rows(
        backward_full_kernel, n, [], taken, weights, each(1, cots) + [wide_kept], 10.0
    )
    taken = [(1, after(cot_late_other, g_kept))] + with_units(f_other)
    *b_other, g_given = over_rows(backward_full_kernel, n, [], taken, *full)
    g_other = send(g_given, core)
    taken = [(1, after(cot_other, b_other[0]))] + with_units(f_early_other)
    *b_early_other, g_early = over_rows(backward_full_kernel, n, [], taken, *full)
    taken = [(1, b_own[0]), (1, after(b_own[1], g_early))]
    (g_own,) = over_rows(backward_rows_kernel, n, [], taken, weights, [wide_kept])
    g_late = halve(g_own, g_other)
    g_early_other = send(after(g_early, g_late), core)
    g_back = send(g_late, plane[-1])
    o_back = after(o_back, g_late)

    def line_sends(lane):
        rows = lane.shape[0] // n_ex
        return [lane[:rows]] + [send(lane[j * rows : (j + 1) * rows], p) for j, p in enumerate(line, 1)]

    steps = max(1, n // BLOCK)
    gate_cots, up_cots, out_cots = zip(b_early, b_early_other, b_own, b_other)

    g_sent = g_late
    parts = (g_kept, g_early_other, g_back)
    for p in reversed(plane[:-1]):
        g_lane, g_sent = split_sum(n_ex, *parts)
        parts = (g_lane, send(g_sent, p))
    lefts = [after(row_lane, g_sent), row_other, row_late, row_late_other]
    gate_grad, up_grad = gradients(lefts, [gate_cots, up_cots], width, steps)
    acts = [after(f_early_own[0], g_sent), f_early_other[0], f_own[0], f_other[0]]
    (down_grad,) = gradients(acts, [out_cots], hidden, steps)
    g_lane = add(parts[0], after(parts[1], gate_grad, down_grad)).astype(BF16)
    g_terms = line_sends(g_lane)
    o_terms = line_sends(add(kept, o_early_other, o_back).astype(BF16))
    parts = (join(after(o_terms[0], g_lane), length=20.0), *o_terms[:0:-1])
    for p in reversed(plane[:-1]):
        lane = add(*parts).astype(BF16)
        half = lane.shape[0] // 2
        parts = (lane[:half], send(lane[half:], p))
    mixed, token_grad = last_sums(parts, [summed(*g_terms[:1], *g_terms[:0:-1], length=10.0)])
    return mixed, token_grad, gate_grad, up_grad, down_grad


def solution(mesh):
    two, three = P(AXES, None), P(AXES, None, None)
    return jax.shard_map(
        body,
        mesh=mesh,
        in_specs=(two, two, two, two, three, three, three),
        out_specs=(two, two, three, three, three),
        check_vma=False,
    )
```

```python
import functools

import jax
import jax.numpy as jnp
from jax import lax
from jax.experimental import pallas as pl
from jax.experimental.pallas import tpu as pltpu
from jax.sharding import PartitionSpec as P

AXES = ("dp", "expert")
F32, BF16 = jnp.float32, jnp.bfloat16
BLOCK = 128


def permutes(n_dp, n_ex):
    def pairs(to):
        out = []
        for d in range(n_dp):
            for z in range(n_ex):
                e, y = to(d, z)
                out.append((d * n_ex + z, e * n_ex + y))
        return out

    def mixed(step, bits):
        def to(d, z):
            bit = step if d % 2 == 0 else bits - 1 - step
            return d ^ (2 << bit), z

        return pairs(to)

    bits = n_dp.bit_length() - 2
    core = pairs(lambda d, z: (d ^ 1, z))
    plane = [mixed(s, bits) for s in range(bits)]
    line = [pairs(lambda d, z, j=j: (d, z ^ j)) for j in reversed(range(1, n_ex))]
    return core, plane, line


def send(x, pairs):
    return lax.ppermute(x, AXES, pairs)


def after(x, *others):
    return lax.optimization_barrier((x, *others))[0]


def add(*terms):
    return functools.reduce(lambda a, b: a + b, [t.astype(F32) for t in terms])


def nt(left, right):
    return lax.dot_general(left, right, (((1,), (1,)), ((), ())), preferred_element_type=F32)


def tn(left, right):
    return lax.dot_general(left, right, (((0,), (0,)), ((), ())), preferred_element_type=F32)


def dot(left, right):
    return jnp.dot(left, right, preferred_element_type=F32)


def shaped(*arrays):
    return [jax.ShapeDtypeStruct(s, t) for s, t in arrays]


def params(mib):
    return pltpu.CompilerParams(vmem_limit_bytes=mib << 20)


def cost(microseconds):
    return pl.CostEstimate(flops=int(microseconds * 1.15e9), bytes_accessed=0, transcendentals=0)


WHOLE = pl.BlockSpec(memory_space=pltpu.VMEM)
ANY = pl.BlockSpec(memory_space=pltpu.HBM)


def payload_kernel(experts, tokens, cotangent, route_in, probs_in, out, cot, route, probs, sems):
    rows, width = tokens.shape
    copies = [
        pltpu.make_async_copy(a, b, sems.at[i])
        for i, (a, b) in enumerate(
            ((route_in, route), (probs_in, probs), (tokens, out.at[:, :width]), (cotangent, cot))
        )
    ]
    for copy in copies:
        copy.start()
    for copy in copies[:2]:
        copy.wait()
    extra = out.shape[1] - width
    column = lax.broadcasted_iota(jnp.int32, (extra, rows), 0)
    named, part = column, jnp.zeros_like(column)
    for _ in range(2):
        over = named >= experts
        named, part = jnp.where(over, named - experts, named), part + over.astype(jnp.int32)
    table = jnp.zeros((extra, rows), F32)
    for k in range(route.shape[0]):
        table = table + jnp.where(route[k : k + 1, :] == named, probs[k : k + 1, :], 0.0)
    high = table.astype(BF16).astype(F32)
    middle = (table - high).astype(BF16).astype(F32)
    low = table - high - middle
    table = jnp.where(part == 0, high, jnp.where(part == 1, middle, low))
    out[:, width:] = jnp.transpose(table).astype(BF16)
    for copy in copies[2:]:
        copy.wait()


def payload(tokens, cotangent, route, probs, experts):
    rows, width = tokens.shape
    extra = -(-3 * experts // 128) * 128
    return pl.pallas_call(
        functools.partial(payload_kernel, experts),
        in_specs=[ANY] * 4,
        out_specs=[WHOLE] * 2,
        out_shape=[pltpu.VMEM((rows, width + extra), BF16), pltpu.VMEM((rows, width), BF16)],
        scratch_shapes=[
            pltpu.VMEM(route.shape[::-1], jnp.int32),
            pltpu.VMEM(probs.shape[::-1], F32),
            pltpu.SemaphoreType.DMA((4,)),
        ],
        compiler_params=params(60),
    )(tokens, cotangent, route.T, probs.T)


def stage_kernel(gate, up, down, tall, wide, sems):
    copies = [
        pltpu.make_async_copy(a.at[0], b, sems.at[i])
        for i, (a, b) in enumerate(((gate, tall.at[0]), (up, tall.at[1]), (down, wide.at[2])))
    ]
    for copy in copies:
        copy.start()
    for i, copy in enumerate(copies):
        copy.wait()
        if i < 2:
            wide[i] = jnp.transpose(tall[i])
        else:
            tall[i] = jnp.transpose(wide[i])


def stage(gate, up, down):
    _, width, hidden = gate.shape
    return pl.pallas_call(
        stage_kernel,
        in_specs=[ANY] * 3,
        out_specs=[WHOLE] * 2,
        out_shape=[pltpu.VMEM((3, width, hidden), BF16), pltpu.VMEM((3, hidden, width), BF16)],
        scratch_shapes=[pltpu.SemaphoreType.DMA((3,))],
        compiler_params=params(52),
    )(gate, up, down)


class Weights:
    def __init__(self, refs):
        self.refs = refs
        self.staged = len(refs) == 2

    def hidden(self, x):
        if self.staged:
            return dot(x, self.refs[0][0]), dot(x, self.refs[0][1])
        return dot(x, self.refs[0][0]), dot(x, self.refs[1][0])

    def out(self, act):
        return dot(act, self.refs[1][2] if self.staged else self.refs[2][0])

    def act_cot(self, out_cot):
        return dot(out_cot, self.refs[0][2]) if self.staged else nt(out_cot, self.refs[2][0])

    def row_cot(self, gate, up):
        if self.staged:
            return dot(gate, self.refs[1][0]) + dot(up, self.refs[1][1])
        return nt(gate, self.refs[0][0]) + nt(up, self.refs[1][0])


def join_kernel(blocks, order, *refs):
    at, out = 0, refs[-1]
    arrays = [refs[i] for i in order] if order else refs[:-1]
    for i in range(blocks):
        for ref in arrays:
            size = ref.shape[0] // blocks
            out[at : at + size, :] = ref[i * size : (i + 1) * size, :]
            at += size


def join(*arrays, blocks=1, order=(), length=0.0):
    rows = sum(a.shape[0] for a in arrays)
    return pl.pallas_call(
        functools.partial(join_kernel, blocks, order),
        in_specs=[WHOLE] * len(arrays),
        out_specs=WHOLE,
        out_shape=pltpu.VMEM((rows, arrays[0].shape[1]), BF16),
        compiler_params=params(4),
        cost_estimate=cost(length),
    )(*arrays)


def split_sum_kernel(blocks, *refs):
    arrays, outs = refs[:-2], refs[-2:]
    half = outs[0].shape[0] // blocks
    for i in range(blocks):
        for j, out in enumerate(outs):
            rows = pl.ds((2 * i + j) * half, half)
            total = functools.reduce(lambda x, y: x + y, [r[rows, :].astype(F32) for r in arrays])
            out[i * half : (i + 1) * half, :] = total.astype(BF16)


def split_sum(blocks, *arrays):
    rows, width = arrays[0].shape
    return pl.pallas_call(
        functools.partial(split_sum_kernel, blocks),
        in_specs=[WHOLE] * len(arrays),
        out_specs=[WHOLE] * 2,
        out_shape=[pltpu.VMEM((rows // 2, width), BF16)] * 2,
        compiler_params=params(4),
        cost_estimate=cost(0.0),
    )(*arrays)


def grid_specs(block, arrays, whole):
    specs = [pl.BlockSpec((block * f, w), lambda i: (i, 0)) for f, w in arrays]
    return specs + [pl.BlockSpec(w.shape, lambda i: (0, 0, 0)) for w in whole]


def sum_kernel(*refs):
    refs[-1][...] = functools.reduce(lambda x, y: x + y, [r[...].astype(F32) for r in refs[:-1]]).astype(BF16)


def summed(*arrays, length=0.0):
    return pl.pallas_call(
        sum_kernel,
        in_specs=[WHOLE] * len(arrays),
        out_specs=WHOLE,
        out_shape=pltpu.VMEM(arrays[0].shape, BF16),
        compiler_params=params(4),
        cost_estimate=cost(length),
    )(*arrays)


def last_sums_kernel(counts, *refs):
    taken, results, held, sems = refs[: sum(counts)], refs[-5:-3], refs[-3:-1], refs[-1]
    copies = []
    for i, count in enumerate(counts):
        total = functools.reduce(lambda x, y: x + y, [r[...].astype(F32) for r in taken[:count]])
        taken = taken[count:]
        held[i][...] = total.astype(BF16)
        copies.append(pltpu.make_async_copy(held[i], results[i], sems.at[i]))
        copies[i].start()
    for copy in copies:
        copy.wait()


def last_sums(*groups):
    shape = groups[0][0].shape
    return pl.pallas_call(
        functools.partial(last_sums_kernel, [len(g) for g in groups]),
        in_specs=[WHOLE] * sum(len(g) for g in groups),
        out_specs=[ANY] * len(groups),
        out_shape=shaped(*[(shape, BF16)] * len(groups)),
        scratch_shapes=[pltpu.VMEM(shape, BF16)] * len(groups) + [pltpu.SemaphoreType.DMA((len(groups),))],
        compiler_params=params(4),
        cost_estimate=cost(0.0),
    )(*[a for g in groups for a in g])


def over_rows(kernel, n, scalars, taken, weights, given, length=0.0):
    block = min(n, BLOCK)
    if block == n:
        call = dict(in_specs=[WHOLE] * (len(taken) + len(weights)), out_specs=[WHOLE] * len(given))
    else:
        call = dict(
            grid=(n // block,),
            in_specs=grid_specs(block, [(f, a.shape[1]) for f, a in taken], weights),
            out_specs=grid_specs(block, [(f, w) for f, w, _ in given], []),
        )
    call["in_specs"] = [pl.BlockSpec(memory_space=pltpu.SMEM)] * len(scalars) + call["in_specs"]
    first = len(scalars) + len(taken)

    def run(*refs):
        kernel(*refs[:first], Weights(refs[first : first + len(weights)]), *refs[first + len(weights) :])

    return pl.pallas_call(
        run,
        out_shape=shaped(*[((f * n, w), t) for f, w, t in given]),
        compiler_params=params(12 if block == n else 40),
        cost_estimate=cost(length),
        **call,
    )(*scalars, *[a for _, a in taken], *weights)


def expert_weight(experts, expert, table):
    column = lax.broadcasted_iota(jnp.int32, table.shape, 1)
    mine = expert[0, 0]
    mine = (column == mine) | (column == mine + experts) | (column == mine + 2 * experts)
    return jnp.sum(jnp.where(mine, table.astype(F32), 0.0), axis=1, keepdims=True)


def hidden_values(x, weights):
    gate, up = weights.hidden(x)
    s = jax.nn.sigmoid(gate)
    gate_s = gate * s
    return (gate_s * up).astype(BF16), up * s * (1.0 + gate * (1.0 - s)), gate_s


def hidden_units(x, weights, act, gate_f, up_f):
    values = hidden_values(x, weights)
    act[...], gate_f[...], up_f[...] = values
    return values[0]


def forward_hidden_kernel(experts, width, expert, a, weights, act, gate_f, up_f, weight):
    weight[...] = jnp.broadcast_to(expert_weight(experts, expert, a[:, width:]), weight.shape)
    hidden_units(a[:, :width], weights, act, gate_f, up_f)


def forward_out_kernel(act, weight, weights, out):
    out[...] = (weight[:, :1] * weights.out(act[...])).astype(out.dtype)


def forward_full_kernel(experts, width, expert, a, weights, act, gate_f, up_f, weight, out):
    p = expert_weight(experts, expert, a[:, width:])
    weight[...] = jnp.broadcast_to(p, weight.shape)
    act_val = hidden_units(a[:, :width], weights, act, gate_f, up_f)
    out[...] = (p * weights.out(act_val)).astype(out.dtype)


def hidden_cots(cot, weight, gate_f, up_f, weights, gate_cot, up_cot, out_cot):
    out = (cot.astype(F32) * weight[:, :1]).astype(BF16)
    out_cot[...] = out
    act_cot = weights.act_cot(out)
    gate = (act_cot * gate_f[...]).astype(BF16)
    up = (act_cot * up_f[...]).astype(BF16)
    gate_cot[...], up_cot[...] = gate, up
    return gate, up


def backward_hidden_kernel(cot, weight, gate_f, up_f, weights, gate_cot, up_cot, out_cot):
    hidden_cots(cot[...], weight, gate_f, up_f, weights, gate_cot, up_cot, out_cot)


def backward_rows_kernel(gate, up, weights, out):
    out[...] = weights.row_cot(gate[...], up[...]).astype(out.dtype)


def backward_full_kernel(cot, weight, gate_f, up_f, weights, gate_cot, up_cot, out_cot, out):
    gate, up = hidden_cots(cot[...], weight, gate_f, up_f, weights, gate_cot, up_cot, out_cot)
    out[...] = weights.row_cot(gate, up).astype(out.dtype)


def chunk_kernel(over_left, chunks, counts, *refs):
    outs = len(counts) - 1
    joined = []
    for count in counts:
        joined.append(refs[:count])
        refs = refs[count:]
    results, held, sems = refs[:outs], refs[outs:-1], refs[-1]
    split = 0 if over_left else 1
    rest = [None if i == split else jnp.concatenate([r[...] for r in group]) for i, group in enumerate(joined)]
    if over_left:
        right = jnp.concatenate(rest[1:], axis=1)
    size = held[0].shape[split] // chunks
    copies = []
    for i in range(chunks):
        part = pl.ds(i * size, size)
        piece = jnp.concatenate([r[:, part] for r in joined[split]])
        value = tn(piece, right) if over_left else tn(rest[0], piece)
        for j in range(outs):
            width = value.shape[1] // outs
            at = (part, slice(None)) if over_left else (slice(None), part)
            held[j][at] = value[:, j * width : (j + 1) * width].astype(BF16)
            copy = pltpu.make_async_copy(held[j].at[at], results[j].at[(0, *at)], sems.at[i, j])
            copy.start()
            copies.append(copy)
    for copy in copies:
        copy.wait()


def gradients_by_chunks(left, rights, width, over_left, chunks=4):
    hidden = rights[0][0].shape[1]
    groups = [left, *rights]
    flat = [piece for group in groups for piece in group]
    return pl.pallas_call(
        functools.partial(chunk_kernel, over_left, chunks, [len(g) for g in groups]),
        in_specs=[WHOLE] * len(flat),
        out_specs=[ANY] * len(rights),
        out_shape=shaped(*[((1, width, hidden), BF16)] * len(rights)),
        scratch_shapes=[pltpu.VMEM((width, hidden), BF16)] * len(rights) + [pltpu.SemaphoreType.DMA((chunks, len(rights)))],
        compiler_params=params(16),
        cost_estimate=cost(10.0),
    )(*flat)


def gradient_kernel(width, counts, *refs):
    joined = []
    for count in counts:
        joined.append(jnp.concatenate([r[...] for r in refs[:count]]))
        refs = refs[count:]
    outs, total = refs[:-1], refs[-1]
    part = tn(joined[0][:, :width], jnp.concatenate(joined[1:], axis=1))

    def write(value):
        hidden = value.shape[1] // len(outs)
        for i, out in enumerate(outs):
            out[0] = value[:, i * hidden : (i + 1) * hidden].astype(BF16)

    if total.shape[0] == 8:
        write(part)
        return
    step = pl.program_id(0)

    @pl.when(step == 0)
    def _():
        total[...] = part

    @pl.when(step > 0)
    def _():
        total[...] += part

    @pl.when(step == pl.num_programs(0) - 1)
    def _():
        write(total[...])


def gradients(left, rights, width, steps):
    hidden = rights[0][0].shape[1]
    if steps == 1:
        over_left = width > hidden
        if max(width, hidden) % (4 * 128) == 0:
            return gradients_by_chunks(left, rights, width, over_left)
    groups = [left, *rights]
    flat = [piece for group in groups for piece in group]
    if steps == 1:
        specs = [WHOLE] * len(flat)
    else:
        specs = [pl.BlockSpec((a.shape[0] // steps, a.shape[1]), lambda i: (i, 0)) for a in flat]
    total = (8, 128) if steps == 1 else (width, len(rights) * hidden)
    return pl.pallas_call(
        functools.partial(gradient_kernel, width, [len(g) for g in groups]),
        grid=(steps,),
        in_specs=specs,
        out_specs=[pl.BlockSpec((1, width, hidden), lambda i: (0, 0, 0))] * len(rights),
        out_shape=shaped(*[((1, width, hidden), BF16)] * len(rights)),
        scratch_shapes=[pltpu.VMEM(total, F32)],
        compiler_params=params(24 if steps == 1 else 48),
        cost_estimate=cost(10.0),
    )(*flat)


def body(tokens, route, probs, cotangent, gate_weight, up_weight, down_weight):
    n_dp, n_ex = lax.axis_size("dp"), lax.axis_size("expert")
    experts = n_dp * n_ex // 2
    rows, width = tokens.shape
    hidden = gate_weight.shape[2]
    core, plane, line = permutes(n_dp, n_ex)
    expert = lax.shift_right_logical(lax.axis_index(AXES).astype(jnp.int32), 1).reshape(1, 1)
    expert, tokens = lax.optimization_barrier((expert, tokens))
    units = [(hidden, BF16), (hidden, F32), (hidden, F32), (128, F32)]
    cots = [(hidden, BF16), (hidden, BF16), (width, BF16)]
    wide, wide_kept = (1, width, BF16), (1, width, F32)

    def each(factor, arrays):
        return [(factor, *a) for a in arrays]

    own, cot = payload(tokens, cotangent, route, probs, experts)
    weights = (gate_weight, up_weight, down_weight)
    staged = n_ex * rows * 2 <= BLOCK
    if staged:
        weights = stage(*(after(w, own) for w in weights))
    for p in plane[:-1]:
        cot = join(cot, send(cot, p))
    row_lane = join(after(own, weights[0], cot), *[send(own, p) for p in line[::-1]], order=(0, *range(len(line), 0, -1)))
    cot = after(cot, row_lane)
    pieces = [send(cot, p) for p in line]
    for p in plane[:-1]:
        row_lane = join(row_lane, send(row_lane, p), blocks=n_ex)
    n = row_lane.shape[0]
    row_late = send(row_lane, plane[-1])
    row_other = send(row_lane, core)

    def forward(kernel, *args):
        return functools.partial(kernel, experts, width), n, [expert], *args

    *f_early_own, kept = over_rows(
        *forward(forward_full_kernel, [(1, row_lane)], weights, each(1, units) + [wide_kept], 10.0)
    )
    order = (0, *range(2, len(line) + 1), 1)
    cot_lane = join(after(cot, kept), *pieces[-1:], *pieces[:-1], order=order, length=10.0)
    cot_late = send(cot_lane, plane[-1])
    cot_other = send(cot_lane, core)

    def halve(kept, received):
        return add(kept, received).astype(BF16)

    def with_units(f):
        return [(1, f[3]), (1, f[1]), (1, f[2])]

    row_late = after(row_late, cot_lane)
    row_late_other = send(row_late, core)
    f_own = over_rows(*forward(forward_hidden_kernel, [(1, row_late)], weights, each(1, units), 10.0))
    full = weights, each(1, units) + [wide], 10.0
    *f_early_other, given = over_rows(*forward(forward_full_kernel, [(1, after(row_other, f_own[0]))], *full))
    row_late_other_in = after(row_late_other, given)
    *f_other, o_given = over_rows(*forward(forward_full_kernel, [(1, row_late_other_in)], *full))
    o_other = send(o_given, core)
    taken = [(1, after(cot_lane, f_other[0]))] + with_units(f_early_own)
    *b_early, g_kept = over_rows(
        backward_full_kernel, n, [], taken, weights, each(1, cots) + [wide_kept], 10.0
    )
    taken = [(1, f_own[0]), (1, after(f_own[3], g_kept))]
    (o_own,) = over_rows(forward_out_kernel, n, [], taken, weights, [wide_kept])
    o_late = halve(o_own, o_other)
    o_early_other = send(given, core)
    o_back = send(o_late, plane[-1])

    cot_late = after(cot_late, o_late)
    cot_late_other = send(cot_late, core)
    taken = [(1, cot_late)] + with_units(f_own)
    b_own = over_rows(backward_hidden_kernel, n, [], taken, weights, each(1, cots), 10.0)
    full = weights, each(1, cots) + [wide], 10.0
    taken = [(1, after(cot_other, b_own[0]))] + with_units(f_early_other)
    *b_early_other, g_early = over_rows(backward_full_kernel, n, [], taken, *full)
    taken = [(1, after(cot_late_other, g_early))] + with_units(f_other)
    *b_other, g_given = over_rows(backward_full_kernel, n, [], taken, *full)
    g_other = send(g_given, core)
    taken = [(1, b_own[0]), (1, after(b_own[1], b_other[0]))]
    (g_own,) = over_rows(backward_rows_kernel, n, [], taken, weights, [wide_kept], 10.0)
    g_late = halve(g_own, g_other)
    g_early_other = send(after(g_early, g_late), core)
    g_back = send(g_late, plane[-1])
    o_back = after(o_back, g_late)

    def line_sends(lane):
        rows = lane.shape[0] // n_ex
        return [lane[:rows]] + [send(lane[j * rows : (j + 1) * rows], p) for j, p in enumerate(line, 1)]

    steps = max(1, n // BLOCK)
    gate_cots, up_cots, out_cots = zip(b_early, b_early_other, b_own, b_other)

    g_sent = g_late
    parts = (g_kept, g_early_other, g_back)
    for p in reversed(plane[:-1]):
        g_lane, g_sent = split_sum(n_ex, *parts)
        parts = (g_lane, send(g_sent, p))
    lefts = [after(row_lane, g_sent), row_other, row_late, row_late_other]
    gate_grad, up_grad = gradients(lefts, [gate_cots, up_cots], width, steps)
    acts = [after(f_early_own[0], g_sent), f_early_other[0], f_own[0], f_other[0]]
    (down_grad,) = gradients(acts, [out_cots], hidden, steps)
    g_lane = add(parts[0], after(parts[1], gate_grad, down_grad)).astype(BF16)
    g_terms = line_sends(g_lane)
    o_terms = line_sends(add(kept, o_early_other, o_back).astype(BF16))
    parts = (join(after(o_terms[0], g_lane), length=20.0), *o_terms[-1:], *o_terms[1:-1])
    for p in reversed(plane[:-1]):
        lane = add(*parts).astype(BF16)
        half = lane.shape[0] // 2
        parts = (lane[:half], send(lane[half:], p))
    mixed, token_grad = last_sums(parts, [summed(*g_terms[:1], *g_terms[:0:-1], length=10.0)])
    return mixed, token_grad, gate_grad, up_grad, down_grad


def solution(mesh):
    two, three = P(AXES, None), P(AXES, None, None)
    return jax.shard_map(
        body,
        mesh=mesh,
        in_specs=(two, two, two, two, three, three, three),
        out_specs=(two, two, three, three, three),
        check_vma=False,
    )
```
